32 devices in a mesh: ctx: 16 (over z, y, core), tp: 2 (over x).
Axes of the slice: x: 2, y: 2, z: 4, core: 2. Of those that a mesh axis runs over, the one named last changes fastest.
Arguments:
- tokens_clean: bfloat16 [2048, 4096], P(('ctx', 'tp')), may hold values from -6 to 6
- noise_mask: int32 [2048], P(('ctx', 'tp')), may hold values 0 or 1
- mask_embed: bfloat16 [4096], replicated, may hold values from -6 to 6
- norm_gain: bfloat16 [4096], replicated, may hold values from 0.099609375 to 1.8984375
- w_query: bfloat16 [4096, 2048], P(None, 'tp'), may hold values from -0.375 to 0.375
- w_key: bfloat16 [4096, 2048], P(None, 'tp'), may hold values from -0.375 to 0.375
- w_value: bfloat16 [4096, 2048], P(None, 'tp'), may hold values from -0.09375 to 0.09375
- w_out: bfloat16 [2048, 4096], P('tp'), may hold values from -0.5 to 0.5
- block_mask: int32 [64, 64], replicated, may hold values from 0 to 3, as said below
Outputs:
- clean_out: bfloat16 [2048, 4096], P(('ctx', 'tp'))
- noisy_out: bfloat16 [2048, 4096], P(('ctx', 'tp'))
The draws below stay inside these ranges and needn't reach their ends.
Inputs may be any that keep to these rules, and one draw needn't show every extreme that they name: `block_mask`: entry (i, j) is a + 2 b: a = 1 where clean block i sees clean block j, b = 1 where noisy block i sees clean block j. For each i the j with a = 1 form one run ending at j = i, and those with b = 1 one run ending at j = i - 1, or none; entries with j > i are 0.
All inputs are finite; a program needn't handle non-finite values. No bound on the sum of `noise_mask` on one device may be relied on, other than what follows from the above.
Results may differ from the reference program's by a relative error of at most 0.014.
Values may be sent and summed in bfloat16 or wider, within the bound.
A program may use at most 128 MiB of HBM per device.

```python
import jax
import jax.numpy as jnp
from jax import lax

D = 4096
HEADS = 16
HEAD_DIM = 128
BLOCK = 32
TOK_DEV = 128
SEQ = 2048
NBLK = 64
N_TP = 2


def pair_weights(key):
    base = jax.random.normal(jax.random.fold_in(key, 11), (D, HEADS * HEAD_DIM), jnp.float32)
    other = jax.random.normal(jax.random.fold_in(key, 12), (D, HEADS * HEAD_DIM), jnp.float32)
    return (base, other)


def draw_w_query(key, part):
    base, other = pair_weights(key)
    weight = base * D ** (-0.5)
    return jnp.clip(weight, -0.375, 0.375).astype(jnp.bfloat16)


def draw_w_key(key, part):
    base, other = pair_weights(key)
    weight = other * D ** (-0.5)
    return jnp.clip(weight, -0.375, 0.375).astype(jnp.bfloat16)


def draw_block_mask(key, part):
    blocks = jnp.arange(NBLK, dtype=jnp.int32)
    clean_start = jax.random.randint(jax.random.fold_in(key, 21), (NBLK,), 0, blocks + 1)
    noisy_start = jax.random.randint(jax.random.fold_in(key, 22), (NBLK,), 0, blocks + 1)
    columns = blocks[None, :]
    clean = (columns >= clean_start[:, None]) & (columns <= blocks[:, None])
    noisy = (columns >= noisy_start[:, None]) & (columns < blocks[:, None])
    return clean.astype(jnp.int32) + 2 * noisy.astype(jnp.int32)


def place_ends(result, key, smallest, largest):
    longest = result.shape.index(max(result.shape))
    spots = []
    for shift in (0, 1):
        where = [jax.random.randint(jax.random.fold_in(key, axis), (), 0, length) for axis, length in enumerate(result.shape)]
        where[longest] = (where[longest] + shift) % result.shape[longest]
        spots.append(tuple(where))
    return result.at[spots[0]].set(smallest).at[spots[1]].set(largest)


def levels(stream_key, dims, cuts, low, high):
    def one(axis_at, blocks):
        draws = jax.random.uniform(jax.random.fold_in(jax.random.fold_in(stream_key, 6), axis_at), (blocks,), jnp.float32, low / len(cuts), high / len(cuts))
        return jnp.repeat(jnp.exp(draws), dims[axis_at] // blocks).reshape((-1,) + (1,) * (len(dims) - axis_at - 1))

    factor_of = one(*cuts[0])
    for cut in cuts[1:]:
        factor_of = factor_of * one(*cut)
    return factor_of


def scatter_about(rng, shape, deviation, reach, shards=(), kind=jnp.bfloat16):
    entries = jax.random.normal(rng, shape, jnp.float32) * deviation
    if len(shards) > 0:
        entries = levels(rng, shape, shards, -0.22, 0.18) * entries
    return jnp.clip(entries, min=-reach, max=reach).astype(kind)


def setup_inputs(seed: int = 0) -> dict:
    seeds = jax.random.split(jax.random.key(seed), 10)
    return {
        "tokens_clean": scatter_about(seeds[0], (SEQ, D), 1.0, 6.0, ((0, 32),)),
        "noise_mask": place_ends((jax.random.randint(seeds[1], (SEQ,), 0, 2) < 1).astype(jnp.int32), jax.random.fold_in(seeds[1], 1), 0, 1),
        "mask_embed": scatter_about(seeds[2], (D,), 1.0, 6.0),
        "norm_gain": jnp.clip(1.0 + 0.18 * jax.random.normal(seeds[3], (D,), jnp.float32), 0.099609375, 1.8984375).astype(jnp.bfloat16),
        "w_query": draw_w_query(jax.random.fold_in(seeds[9], 71), 0),
        "w_key": draw_w_key(jax.random.fold_in(seeds[9], 71), 0),
        "w_value": scatter_about(seeds[6], (D, HEADS * HEAD_DIM), D ** -0.5, 0.09375, ((1, 2),)),
        "w_out": scatter_about(seeds[7], (HEADS * HEAD_DIM, D), HEAD_DIM ** -0.5, 0.5, ((0, 2),)),
        "block_mask": draw_block_mask(jax.random.fold_in(seeds[9], 71), 0),
    }


ROPE_BASE = 500000.0
EPSILON = 1e-05

def rms_rows(values, gain):
    wide = values.astype(jnp.float32)
    factor = lax.rsqrt(lax.optimization_barrier(jnp.mean(wide * wide, axis=-1, keepdims=True)) + EPSILON)
    return (wide * factor * gain.astype(jnp.float32)).astype(jnp.bfloat16)

def rotate(values, positions):
    half_dim = values.shape[-1] // 2
    indices = jnp.arange(half_dim).astype(jnp.float32)
    freqs = ROPE_BASE ** (-2.0 * indices / values.shape[-1])
    angles = positions.astype(jnp.float32)[:, None] * freqs[None, :]
    cosine = jnp.cos(angles)[:, None, :]
    sine = jnp.sin(angles)[:, None, :]
    lower = values[..., :half_dim]
    upper = values[..., half_dim:]
    return jnp.concatenate([lower * cosine - upper * sine, upper * cosine + lower * sine], axis=-1)

def widen(values):
    return lax.optimization_barrier(values).astype(jnp.float32)

def mixed_softmax(scores, visible, values):
    masked = jnp.where(visible, scores, -jnp.inf)
    peak = lax.optimization_barrier(jnp.max(masked, axis=-1, keepdims=True))
    weights = jnp.where(visible, jnp.exp(scores - peak), 0.0)
    total = lax.optimization_barrier(jnp.sum(weights, axis=-1))
    weighted = jnp.einsum('hqk,khd->hqd', widen(weights.astype(jnp.bfloat16)), values)
    return jnp.transpose(weighted / total[..., None], (1, 0, 2))

def reference(tokens_clean, noise_mask, mask_embed, norm_gain, w_query, w_key, w_value, w_out, block_mask):
    normed = rms_rows(tokens_clean, norm_gain)
    mask_row = rms_rows(mask_embed[None, :], norm_gain)
    noisy_rows = (noise_mask == 1)[:, None]
    positions = jnp.arange(SEQ, dtype=jnp.int32)

    def project(weight, rotary):
        clean = jnp.dot(normed, weight, preferred_element_type=jnp.float32)
        masked = jnp.dot(mask_row, weight, preferred_element_type=jnp.float32)
        noisy = jnp.where(noisy_rows, masked, clean)
        clean = clean.reshape(SEQ, HEADS, HEAD_DIM)
        noisy = noisy.reshape(SEQ, HEADS, HEAD_DIM)
        if rotary:
            clean = rotate(clean, positions)
            noisy = rotate(noisy, positions)
        return (widen(clean.astype(jnp.bfloat16)), widen(noisy.astype(jnp.bfloat16)))
    q_clean, q_noisy = project(w_query, True)
    k_clean, k_noisy = project(w_key, True)
    v_clean, v_noisy = project(w_value, False)
    score_scale = HEAD_DIM ** (-0.5)
    key_blocks = positions // BLOCK

    def one_block(index):
        begin = index * TOK_DEV
        query_blocks = (begin + jnp.arange(TOK_DEV, dtype=jnp.int32)) // BLOCK
        table = jnp.take(block_mask, query_blocks, axis=0)
        visible = jnp.take(table, key_blocks, axis=1)
        clean_seen = visible % 2 == 1
        noisy_seen = visible // 2 == 1
        own_block = query_blocks[:, None] == query_blocks[None, :]
        query_clean = lax.dynamic_slice_in_dim(q_clean, begin, TOK_DEV, 0)
        query_noisy = lax.dynamic_slice_in_dim(q_noisy, begin, TOK_DEV, 0)
        key_own = lax.dynamic_slice_in_dim(k_noisy, begin, TOK_DEV, 0)
        value_own = lax.dynamic_slice_in_dim(v_noisy, begin, TOK_DEV, 0)
        clean_scores = jnp.einsum('qhd,khd->hqk', query_clean, k_clean) * score_scale
        out_clean = mixed_softmax(clean_scores, clean_seen[None], v_clean)
        noisy_scores = jnp.concatenate([jnp.einsum('qhd,khd->hqk', query_noisy, k_clean), jnp.einsum('qhd,khd->hqk', query_noisy, key_own)], axis=-1) * score_scale
        noisy_visible = jnp.concatenate([noisy_seen, own_block], axis=-1)[None]
        noisy_values = jnp.concatenate([v_clean, value_own], axis=0)
        out_noisy = mixed_softmax(noisy_scores, noisy_visible, noisy_values)
        return (out_clean.reshape(TOK_DEV, HEADS * HEAD_DIM).astype(jnp.bfloat16), out_noisy.reshape(TOK_DEV, HEADS * HEAD_DIM).astype(jnp.bfloat16))
    outs_clean, outs_noisy = lax.map(one_block, jnp.arange(SEQ // TOK_DEV, dtype=jnp.int32))
    outs_clean = outs_clean.reshape(SEQ, HEADS * HEAD_DIM)
    outs_noisy = outs_noisy.reshape(SEQ, HEADS * HEAD_DIM)
    group_width = HEADS * HEAD_DIM // N_TP

    def project_out(attended):
        total = jnp.zeros((SEQ, D), jnp.float32)
        for group in range(N_TP):
            part = jnp.dot(attended[:, group * group_width:(group + 1) * group_width], w_out[group * group_width:(group + 1) * group_width, :], preferred_element_type=jnp.float32)
            total = total + widen(part.astype(jnp.bfloat16))
        return total.astype(jnp.bfloat16)
    return (project_out(outs_clean), project_out(outs_noisy))
```

```python
import functools

import jax
import jax.numpy as jnp
from jax import lax
from jax.experimental import pallas as pl
from jax.experimental.pallas import tpu as pltpu
from jax.sharding import PartitionSpec as P

HEAD_DIM = 128
BLOCK = 32


ROPE_BASE = 500000.0
EPSILON = 1e-05
NEG_FILL = -1e30


def rms_rows(values, gain):
    wide = values.astype(jnp.float32)
    factor = lax.rsqrt(jnp.mean(wide * wide, axis=-1, keepdims=True) + EPSILON)
    return (wide * factor * gain.astype(jnp.float32)).astype(jnp.bfloat16)


def rotate(values, positions):
    half_dim = values.shape[-1] // 2
    indices = jnp.arange(half_dim).astype(jnp.float32)
    freqs = ROPE_BASE ** (-2.0 * indices / values.shape[-1])
    angles = positions.astype(jnp.float32)[:, None] * freqs[None, :]
    cosine = jnp.cos(angles)[:, None, :]
    sine = jnp.sin(angles)[:, None, :]
    lower = values[..., :half_dim]
    upper = values[..., half_dim:]
    return jnp.concatenate([lower * cosine - upper * sine, upper * cosine + lower * sine], axis=-1)


def start_state(heads, length):
    return (
        jnp.full((heads, length), NEG_FILL, jnp.float32),
        jnp.zeros((heads, length), jnp.float32),
        jnp.zeros((heads, length, HEAD_DIM), jnp.float32),
    )


def attend(state, queries, keys, values, visible):
    peak_old, total_old, weighted_old = state
    scores = jnp.einsum(
        "qhd,khd->hqk", queries, keys, preferred_element_type=jnp.float32
    ) * HEAD_DIM ** (-0.5)
    scores = jnp.where(visible[None], scores, NEG_FILL)
    peak_new = jnp.maximum(peak_old, jnp.max(scores, axis=-1))
    weights = jnp.where(visible[None], jnp.exp(scores - peak_new[..., None]), 0.0)
    factor = jnp.exp(peak_old - peak_new)
    total_new = total_old * factor + jnp.sum(weights, axis=-1)
    weighted_new = weighted_old * factor[..., None] + jnp.einsum(
        "hqk,khd->hqd", weights.astype(jnp.bfloat16), values, preferred_element_type=jnp.float32
    )
    return (peak_new, total_new, weighted_new)


def local(
    tokens_clean, noise_mask, mask_embed, norm_gain, w_query, w_key, w_value, w_out, block_mask
):
    normed = rms_rows(tokens_clean, norm_gain)
    mask_row = rms_rows(mask_embed[None, :], norm_gain)
    gathered, noise_flags = (
        lax.all_gather(normed, "tp", axis=0, tiled=True),
        lax.all_gather(noise_mask, "tp", axis=0, tiled=True),
    )
    local_len = gathered.shape[0]
    width = w_query.shape[1]
    heads = width // HEAD_DIM
    first_row = lax.axis_index("ctx") * local_len
    positions = first_row + jnp.arange(local_len, dtype=jnp.int32)
    noisy_rows = (noise_flags == 1)[:, None]

    def project(weight, rotary):
        clean = jnp.dot(gathered, weight, preferred_element_type=jnp.float32)
        masked = jnp.dot(mask_row, weight, preferred_element_type=jnp.float32)
        noisy = jnp.where(noisy_rows, masked, clean)
        clean = clean.reshape(local_len, heads, HEAD_DIM)
        noisy = noisy.reshape(local_len, heads, HEAD_DIM)
        if rotary:
            clean = rotate(clean, positions)
            noisy = rotate(noisy, positions)
        return (clean.astype(jnp.bfloat16), noisy.astype(jnp.bfloat16))

    q_clean, q_noisy = project(w_query, True)
    k_clean, k_noisy = project(w_key, True)
    v_clean, v_noisy = project(w_value, False)
    key_values = jnp.stack([k_clean.reshape(local_len, width), v_clean.reshape(local_len, width)])

    def finish(state):
        weighted = state[2] / state[1][..., None]
        return jnp.transpose(weighted, (1, 0, 2)).reshape(local_len, width).astype(jnp.bfloat16)

    row_table = jnp.take(block_mask, positions // BLOCK, axis=0)
    own_block = (positions // BLOCK)[:, None] == (positions // BLOCK)[None, :]
    noisy_state = attend(start_state(heads, local_len), q_noisy, k_noisy, v_noisy, own_block)
    states = (start_state(heads, local_len), noisy_state)
    piece = lax.all_gather(key_values, "ctx", axis=1, tiled=True)
    count = piece.shape[1]
    visible = jnp.repeat(row_table, BLOCK, axis=1)
    keys = piece[0].reshape(count, heads, HEAD_DIM)
    values = piece[1].reshape(count, heads, HEAD_DIM)
    states = (
        attend(states[0], q_clean, keys, values, visible % 2 == 1),
        attend(states[1], q_noisy, keys, values, visible // 2 == 1),
    )
    attended = jnp.stack([finish(states[0]), finish(states[1])])
    model_width = w_out.shape[1]
    piece = attended
    summed = lax.psum_scatter(
        jnp.einsum("sqc,cd->qsd", piece, w_out, preferred_element_type=jnp.float32)
        .reshape(local_len // lax.axis_size("tp") * lax.axis_size("tp"), 2 * model_width)
        .astype(jnp.bfloat16),
        "tp",
        scatter_dimension=0,
        tiled=True,
    ).astype(jnp.float32)
    result = summed.reshape(summed.shape[0], 2, model_width)
    return (result[:, 0].astype(jnp.bfloat16), result[:, 1].astype(jnp.bfloat16))

LOG2E = 1.4426950408889634
MESH = pl.DeviceIdType.MESH


def layer_kernel(
    n_chips,
    x_ref, flag_ref, mask_ref, gain_ref, cos_ref, sin_ref, vis_ref, wq_hbm, wk_hbm, wv_hbm, wo_hbm,
    clean_ref, noisy_ref,
    w_s, wo_s, lhs0, lhs1, flag0, flag1, mproj, nb, send, recv, kall, vall, bias,
    oown, lown, obuf, lbuf, oin, lin, att, psend, precv, pown,
    wsem, wosem, xs, xr, ss, sr, ls, fs, fr, os_, or_, ol, ps, pr,
):
    ctx = lax.axis_index("ctx")
    tp = lax.axis_index("tp")
    chip = ctx // 2
    core = ctx % 2
    rows = x_ref.shape[0]
    length = 2 * rows
    pairs = n_chips // 2
    hd = HEAD_DIM
    seq = 2 * n_chips * length
    my_z = chip // 2
    w_hbm = (wq_hbm, wk_hbm, wv_hbm)

    def pair_at(i):
        return (my_z + 2 + i) % pairs

    def w_copy(kind, i):
        cols = pl.ds(pl.multiple_of(pair_at(i) * 2 * hd, 2 * hd), 2 * hd)
        return pltpu.make_async_copy(w_hbm[kind].at[:, cols], w_s.at[kind, :, cols], wsem.at[i, kind])

    for i in range(pairs):
        for kind in range(3):
            w_copy(kind, i).start()
    wo_copy = pltpu.make_async_copy(wo_hbm, wo_s, wosem)
    wo_copy.start()

    barrier = pltpu.get_barrier_semaphore()
    pl.semaphore_signal(barrier, inc=1, device_id={"tp": 1 - tp}, device_id_type=MESH)
    pl.semaphore_signal(barrier, inc=1, device_id={"ctx": 2 * chip + 1 - core}, device_id_type=MESH)
    for d in range(1, n_chips):
        peer = (chip + d) % n_chips
        pl.semaphore_signal(barrier, inc=1, device_id={"ctx": 2 * peer + core}, device_id_type=MESH)

    gain = gain_ref[...].astype(jnp.float32)

    def norm(values):
        wide = values.astype(jnp.float32)
        factor = lax.rsqrt(jnp.mean(wide * wide, axis=-1, keepdims=True) + EPSILON)
        return (wide * factor * gain).astype(jnp.bfloat16)

    lhs0[0:rows, :] = norm(x_ref[...])
    lhs0[rows:rows + 16, :] = jnp.broadcast_to(norm(mask_ref[...]), (16, lhs0.shape[1]))
    flag0[...] = jnp.broadcast_to(flag_ref[...].astype(jnp.float32), flag0.shape)

    pl.semaphore_wait(barrier, n_chips + 1)

    def x_copy():
        return pltpu.make_async_remote_copy(
            src_ref=lhs0.at[pl.ds(0, rows)], dst_ref=lhs1, send_sem=xs.at[0], recv_sem=xr.at[0],
            device_id={"tp": 1 - tp}, device_id_type=MESH)

    def flag_copy():
        return pltpu.make_async_remote_copy(
            src_ref=flag0, dst_ref=flag1, send_sem=xs.at[1], recv_sem=xr.at[1],
            device_id={"tp": 1 - tp}, device_id_type=MESH)

    flag_copy().start()
    x_copy().start()

    def half_rows(half):
        which = tp if half == 0 else 1 - tp
        return pl.ds(pl.multiple_of(which * rows, rows), rows)

    def block_copy(head, half):
        where = half_rows(half)
        return pltpu.make_async_remote_copy(
            src_ref=send.at[head, where], dst_ref=recv.at[chip, where],
            send_sem=ss.at[head, half], recv_sem=sr.at[chip, half],
            device_id={"ctx": 2 * head + core}, device_id_type=MESH)

    def block_arrival(source, half):
        where = half_rows(half)
        return pltpu.make_async_remote_copy(
            src_ref=send.at[source, where], dst_ref=recv.at[source, where],
            send_sem=ss.at[source, half], recv_sem=sr.at[source, half],
            device_id={"ctx": 2 * source + core}, device_id_type=MESH)

    def block_here(half):
        where = half_rows(half)
        return pltpu.make_async_copy(send.at[chip, where], recv.at[chip, where], ls.at[half])

    key_at = lax.broadcasted_iota(jnp.int32, (vis_ref.shape[1], seq), 1)
    side = (key_at % (2 * length)) // length
    key_ctx = 2 * (key_at // (2 * length)) + jnp.where(side == 0, core, 1 - core)
    key_block = key_ctx * (length // BLOCK) + (key_at % length) // BLOCK
    spread = (lax.broadcasted_iota(jnp.int32, key_at.shape, 0) == key_block).astype(jnp.float32).astype(jnp.bfloat16)
    shown = jnp.dot(vis_ref[...], spread, preferred_element_type=jnp.float32)
    bias[...] = ((shown - 1.0) * 1e30).reshape(bias.shape)

    for half in range(2):
        if half == 1:
            flag_copy().wait_recv()
            x_copy().wait_recv()
        where = half_rows(half)

        def project(i, carry):
            pair = pair_at(i)
            cols = pl.ds(pl.multiple_of(pair * 2 * hd, 2 * hd), 2 * hd)
            if half == 0:
                for kind in range(3):
                    w_copy(kind, i).wait()
            flags = (flag0 if half == 0 else flag1)[...]
            cosine = cos_ref[half]
            sine = sin_ref[half]
            for kind in range(3):
                left = (lhs0 if half == 0 else lhs1)[...]
                result = jnp.dot(left, w_s[kind, :, cols], preferred_element_type=jnp.float32)
                if half == 0:
                    mproj[kind, :, cols] = result[rows:rows + 8]
                    masked = result[rows:rows + 1]
                else:
                    masked = mproj[kind, :, cols][0:1]
                clean2 = result[0:rows]
                for k in range(2):
                    head = 2 * pair + k
                    clean = clean2[:, k * hd:(k + 1) * hd]
                    noisy = jnp.where(flags == 1.0, masked[:, k * hd:(k + 1) * hd], clean)
                    if kind < 2:
                        clean = clean * cosine + pltpu.roll(clean, hd // 2, 1) * sine
                        noisy = noisy * cosine + pltpu.roll(noisy, hd // 2, 1) * sine
                    clean = clean.astype(jnp.bfloat16)
                    noisy = noisy.astype(jnp.bfloat16)
                    nb[kind, head, where, :] = noisy
                    if kind == 0:
                        send[head, where, 0:hd] = clean
                        send[head, where, hd:2 * hd] = noisy
                    else:
                        send[head, where, (kind + 1) * hd:(kind + 2) * hd] = clean
            for k in range(2):
                head = 2 * pair + k

                @pl.when(head != chip)
                def _():
                    block_copy(head, half).start()

                @pl.when(head == chip)
                def _():
                    block_here(half).start()
            return carry

        lax.fori_loop(0, pairs, project, 0)

    scale = LOG2E * hd ** -0.5
    own = (lax.broadcasted_iota(jnp.int32, (length, length), 0) // BLOCK
           == lax.broadcasted_iota(jnp.int32, (length, length), 1) // BLOCK)

    def dot_t(a, b):
        return lax.dot_general(a, b, (((1,), (1,)), ((), ())), preferred_element_type=jnp.float32)

    for head in range(n_chips):
        scores = jnp.where(own, dot_t(nb[0, head], nb[1, head]) * scale, NEG_FILL)
        peak = jnp.max(scores, axis=-1, keepdims=True)
        weights = jnp.exp2(scores - peak)
        total = jnp.sum(weights, axis=-1, keepdims=True)
        oown[head] = jnp.dot(weights.astype(jnp.bfloat16), nb[2, head], preferred_element_type=jnp.float32) / total
        lown[head] = jnp.broadcast_to(peak + jnp.log(total) * LOG2E, (length, hd))

    def share(p, kind):
        return pltpu.make_async_remote_copy(
            src_ref=recv.at[p, :, pl.ds((2 + kind) * hd, hd)],
            dst_ref=(kall, vall)[kind].at[p, pl.ds(length, length)],
            send_sem=fs.at[p, kind], recv_sem=fr.at[p, kind],
            device_id={"ctx": 2 * chip + 1 - core}, device_id_type=MESH)

    def back(p, kind, slot):
        src = (obuf, lbuf)[kind].at[p]
        dst = (oin, lin)[kind].at[slot]
        return pltpu.make_async_remote_copy(
            src_ref=src, dst_ref=dst, send_sem=os_.at[p, kind], recv_sem=or_.at[slot, kind],
            device_id={"ctx": 2 * p + core}, device_id_type=MESH)

    def back_here(kind):
        return pltpu.make_async_copy((obuf, lbuf)[kind].at[chip], (oin, lin)[kind].at[chip], ol.at[kind])

    for p in range(n_chips):
        for half in range(2):
            @pl.when(chip != p)
            def _():
                block_arrival(p, half).wait_recv()

            @pl.when(chip == p)
            def _():
                block_here(half).wait()
        for kind in range(2):
            share(p, kind).start()
        kall[p, 0:length, :] = recv[p, :, 2 * hd:3 * hd]
        vall[p, 0:length, :] = recv[p, :, 3 * hd:4 * hd]

    for p in range(n_chips):
        for kind in range(2):
            share(p, kind).wait_recv()
        count = (p + 1) * 2 * length
        keys = kall[0:p + 1].reshape(count, hd)
        values = vall[0:p + 1].reshape(count, hd)
        shown = bias[2 * p + core]
        per = length // BLOCK
        for copy in range(2):
            queries = recv[p, :, copy * hd:(copy + 1) * hd]
            extra = jnp.concatenate(
                [jnp.broadcast_to(shown[copy * per + b:copy * per + b + 1, 0:count], (BLOCK, count)) for b in range(per)], axis=0)
            scores = dot_t(queries, keys) * scale + extra
            peak = jnp.max(scores, axis=-1, keepdims=True)
            weights = jnp.exp2(scores - peak)
            total = jnp.sum(weights, axis=-1, keepdims=True)
            result = jnp.dot(weights.astype(jnp.bfloat16), values, preferred_element_type=jnp.float32) / total
            obuf[p, copy * length:(copy + 1) * length, :] = result.astype(jnp.bfloat16)
            if copy == 1:
                level = jnp.broadcast_to(peak + jnp.log(total) * LOG2E, (length, hd))
                lbuf[p] = jnp.transpose(level)[0:8]
        for kind in range(2):
            @pl.when(chip != p)
            def _():
                back(p, kind, chip).start()

            @pl.when(chip == p)
            def _():
                back_here(kind).start()

    mine = pl.ds(pl.multiple_of(tp * rows, rows), rows)
    theirs = pl.ds(pl.multiple_of((1 - tp) * rows, rows), rows)
    for head in range(n_chips):
        for kind in range(2):
            @pl.when(chip != head)
            def _():
                back(head, kind, head).wait_recv()

            @pl.when(chip == head)
            def _():
                back_here(kind).wait()
        away = jnp.transpose(jnp.broadcast_to(lin[head][0:1], (length, hd)))
        home = lown[head]
        top = jnp.maximum(away, home)
        w_away = jnp.exp2(away - top)
        w_home = jnp.exp2(home - top)
        noisy = oin[head, length:2 * length].astype(jnp.float32)
        noisy = (noisy * w_away + oown[head] * w_home) / (w_away + w_home)
        oin[head, length:2 * length] = noisy.astype(jnp.bfloat16)
        cols = slice(head * hd, (head + 1) * hd)
        noisy_at = (pl.ds(pl.multiple_of(length + tp * rows, rows), rows),
                    pl.ds(pl.multiple_of(length + (1 - tp) * rows, rows), rows))
        att[0, 0:rows, cols] = oin[head, mine, :]
        att[1, 0:rows, cols] = oin[head, theirs, :]
        att[0, rows:length, cols] = oin[head, noisy_at[0], :]
        att[1, rows:length, cols] = oin[head, noisy_at[1], :]

    wo_copy.wait()
    chunks = psend.shape[0]
    width = psend.shape[2]

    def term_copy(j):
        return pltpu.make_async_remote_copy(
            src_ref=psend.at[j], dst_ref=precv.at[j], send_sem=ps.at[j], recv_sem=pr.at[j],
            device_id={"tp": 1 - tp}, device_id_type=MESH)

    def out_cols(j):
        return pl.ds(pl.multiple_of(j * width, width), width)

    def term(j, carry):
        psend[j] = jnp.dot(att[1], wo_s[:, out_cols(j)], preferred_element_type=jnp.float32).astype(jnp.bfloat16)
        term_copy(j).start()
        return carry

    lax.fori_loop(0, chunks, term, 0)

    def own_term(j, carry):
        pown[j] = jnp.dot(att[0], wo_s[:, out_cols(j)], preferred_element_type=jnp.float32).astype(jnp.bfloat16)
        return carry

    lax.fori_loop(0, chunks, own_term, 0)

    def total_of(j, carry):
        term_copy(j).wait_recv()
        summed = (pown[j].astype(jnp.float32) + precv[j].astype(jnp.float32)).astype(jnp.bfloat16)
        clean_ref[:, out_cols(j)] = summed[0:rows]
        noisy_ref[:, out_cols(j)] = summed[rows:length]
        return carry

    lax.fori_loop(0, chunks, total_of, 0)

    flag_copy().wait_send()
    x_copy().wait_send()
    for p in range(n_chips):
        for kind in range(2):
            share(p, kind).wait_send()

        @pl.when(chip != p)
        def _():
            for half in range(2):
                block_copy(p, half).wait_send()
            for kind in range(2):
                back(p, kind, chip).wait_send()
    for j in range(chunks):
        term_copy(j).wait_send()


def local_kernel(
    tokens_clean, noise_mask, mask_embed, norm_gain, w_query, w_key, w_value, w_out, block_mask
):
    rows, model = tokens_clean.shape
    length = 2 * rows
    width = w_query.shape[1]
    n_chips = width // HEAD_DIM
    hd = HEAD_DIM
    seq = 2 * n_chips * length
    n_blocks = block_mask.shape[0]
    per = length // BLOCK
    ctx = lax.axis_index("ctx")
    tp = lax.axis_index("tp")
    indices = jnp.arange(hd // 2).astype(jnp.float32)
    freqs = ROPE_BASE ** (-2.0 * indices / hd)
    starts = ctx * length + jnp.stack([tp, 1 - tp]) * rows
    positions = starts[:, None] + jnp.arange(rows, dtype=jnp.int32)[None, :]
    angles = positions.astype(jnp.float32)[..., None] * freqs
    cosine = jnp.cos(angles)
    sine = jnp.sin(angles)
    cosine = jnp.concatenate([cosine, cosine], axis=-1)
    sine = jnp.concatenate([-sine, sine], axis=-1)
    table = block_mask.reshape(n_blocks // per, per, n_blocks)
    seen = jnp.concatenate([table % 2, table // 2], axis=1).reshape(2 * n_blocks, n_blocks).astype(jnp.bfloat16)
    bf, f32 = jnp.bfloat16, jnp.float32
    chunks = 8
    part = model // chunks
    dma = pltpu.SemaphoreType.DMA
    vmem = pl.BlockSpec(memory_space=pltpu.VMEM)
    hbm = pl.BlockSpec(memory_space=pl.ANY)
    return pl.pallas_call(
        functools.partial(layer_kernel, n_chips),
        out_shape=(jax.ShapeDtypeStruct((rows, model), bf), jax.ShapeDtypeStruct((rows, model), bf)),
        in_specs=[vmem] * 7 + [hbm] * 4,
        out_specs=(vmem, vmem),
        scratch_shapes=[
            pltpu.VMEM((3, model, width), bf),
            pltpu.VMEM((width, model), bf),
            pltpu.VMEM((rows + 16, model), bf),
            pltpu.VMEM((rows, model), bf),
            pltpu.VMEM((rows, hd), f32),
            pltpu.VMEM((rows, hd), f32),
            pltpu.VMEM((3, 8, width), f32),
            pltpu.VMEM((3, n_chips, length, hd), bf),
            pltpu.VMEM((n_chips, length, 4 * hd), bf),
            pltpu.VMEM((n_chips, length, 4 * hd), bf),
            pltpu.VMEM((n_chips, 2 * length, hd), bf),
            pltpu.VMEM((n_chips, 2 * length, hd), bf),
            pltpu.VMEM((2 * n_chips, 2 * per, seq), f32),
            pltpu.VMEM((n_chips, length, hd), f32),
            pltpu.VMEM((n_chips, length, hd), f32),
            pltpu.VMEM((n_chips, 2 * length, hd), bf),
            pltpu.VMEM((n_chips, 8, hd), f32),
            pltpu.VMEM((n_chips, 2 * length, hd), bf),
            pltpu.VMEM((n_chips, 8, hd), f32),
            pltpu.VMEM((2, length, width), bf),
            pltpu.VMEM((chunks, length, part), bf),
            pltpu.VMEM((chunks, length, part), bf),
            pltpu.VMEM((chunks, length, part), bf),
            dma((n_chips // 2, 3)),
            dma,
            dma((2,)),
            dma((2,)),
            dma((n_chips, 2)),
            dma((n_chips, 2)),
            dma((2,)),
            dma((n_chips, 2)),
            dma((n_chips, 2)),
            dma((n_chips, 2)),
            dma((n_chips, 2)),
            dma((2,)),
            dma((chunks,)),
            dma((chunks,)),
        ],
        compiler_params=pltpu.CompilerParams(
            collective_id=0, has_side_effects=True, vmem_limit_bytes=60 * 1024 * 1024),
        cost_estimate=pl.CostEstimate(flops=6 * 10**9, bytes_accessed=34 * 2**20, transcendentals=3 * 10**6),
    )(tokens_clean, noise_mask.reshape(rows, 1), mask_embed.reshape(1, model), norm_gain.reshape(1, model),
      cosine, sine, seen, w_query, w_key, w_value, w_out)


def fits(mesh, tokens_clean, w_query):
    n_ctx, n_tp = mesh.shape["ctx"], mesh.shape["tp"]
    heads = w_query.shape[1] // n_tp // HEAD_DIM
    tokens = tokens_clean.shape[0] // n_ctx
    return n_tp == 2 and n_ctx == 2 * heads and heads % 4 == 0 and tokens == HEAD_DIM


def solution(mesh):
    specs = dict(
        mesh=mesh,
        in_specs=(
            P(("ctx", "tp"), None),
            P(("ctx", "tp")),
            P(),
            P(),
            P(None, "tp"),
            P(None, "tp"),
            P(None, "tp"),
            P("tp", None),
            P(),
        ),
        out_specs=(P(("ctx", "tp"), None), P(("ctx", "tp"), None)),
        check_vma=False,
    )

    def layer(tokens_clean, noise_mask, mask_embed, norm_gain, w_query, w_key, w_value, w_out, block_mask):
        body = local_kernel if fits(mesh, tokens_clean, w_query) else local
        return jax.shard_map(body, **specs)(
            tokens_clean, noise_mask, mask_embed, norm_gain, w_query, w_key, w_value, w_out, block_mask)

    return layer
```

```python
import functools

import jax
import jax.numpy as jnp
import numpy as np
from jax import lax
from jax.experimental import pallas as pl
from jax.experimental.pallas import tpu as pltpu
from jax.sharding import PartitionSpec as P

HEAD_DIM = 128
BLOCK = 32


ROPE_BASE = 500000.0
EPSILON = 1e-05
NEG_FILL = -1e30


def rms_rows(values, gain):
    wide = values.astype(jnp.float32)
    factor = lax.rsqrt(jnp.mean(wide * wide, axis=-1, keepdims=True) + EPSILON)
    return (wide * factor * gain.astype(jnp.float32)).astype(jnp.bfloat16)


def rotate(values, positions):
    half_dim = values.shape[-1] // 2
    indices = jnp.arange(half_dim).astype(jnp.float32)
    freqs = ROPE_BASE ** (-2.0 * indices / values.shape[-1])
    angles = positions.astype(jnp.float32)[:, None] * freqs[None, :]
    cosine = jnp.cos(angles)[:, None, :]
    sine = jnp.sin(angles)[:, None, :]
    lower = values[..., :half_dim]
    upper = values[..., half_dim:]
    return jnp.concatenate([lower * cosine - upper * sine, upper * cosine + lower * sine], axis=-1)


def start_state(heads, length):
    return (
        jnp.full((heads, length), NEG_FILL, jnp.float32),
        jnp.zeros((heads, length), jnp.float32),
        jnp.zeros((heads, length, HEAD_DIM), jnp.float32),
    )


def attend(state, queries, keys, values, visible):
    peak_old, total_old, weighted_old = state
    scores = jnp.einsum(
        "qhd,khd->hqk", queries, keys, preferred_element_type=jnp.float32
    ) * HEAD_DIM ** (-0.5)
    scores = jnp.where(visible[None], scores, NEG_FILL)
    peak_new = jnp.maximum(peak_old, jnp.max(scores, axis=-1))
    weights = jnp.where(visible[None], jnp.exp(scores - peak_new[..., None]), 0.0)
    factor = jnp.exp(peak_old - peak_new)
    total_new = total_old * factor + jnp.sum(weights, axis=-1)
    weighted_new = weighted_old * factor[..., None] + jnp.einsum(
        "hqk,khd->hqd", weights.astype(jnp.bfloat16), values, preferred_element_type=jnp.float32
    )
    return (peak_new, total_new, weighted_new)


def local(
    tokens_clean, noise_mask, mask_embed, norm_gain, w_query, w_key, w_value, w_out, block_mask
):
    normed = rms_rows(tokens_clean, norm_gain)
    mask_row = rms_rows(mask_embed[None, :], norm_gain)
    gathered, noise_flags = (
        lax.all_gather(normed, "tp", axis=0, tiled=True),
        lax.all_gather(noise_mask, "tp", axis=0, tiled=True),
    )
    local_len = gathered.shape[0]
    width = w_query.shape[1]
    heads = width // HEAD_DIM
    first_row = lax.axis_index("ctx") * local_len
    positions = first_row + jnp.arange(local_len, dtype=jnp.int32)
    noisy_rows = (noise_flags == 1)[:, None]

    def project(weight, rotary):
        clean = jnp.dot(gathered, weight, preferred_element_type=jnp.float32)
        masked = jnp.dot(mask_row, weight, preferred_element_type=jnp.float32)
        noisy = jnp.where(noisy_rows, masked, clean)
        clean = clean.reshape(local_len, heads, HEAD_DIM)
        noisy = noisy.reshape(local_len, heads, HEAD_DIM)
        if rotary:
            clean = rotate(clean, positions)
            noisy = rotate(noisy, positions)
        return (clean.astype(jnp.bfloat16), noisy.astype(jnp.bfloat16))

    q_clean, q_noisy = project(w_query, True)
    k_clean, k_noisy = project(w_key, True)
    v_clean, v_noisy = project(w_value, False)
    key_values = jnp.stack([k_clean.reshape(local_len, width), v_clean.reshape(local_len, width)])

    def finish(state):
        weighted = state[2] / state[1][..., None]
        return jnp.transpose(weighted, (1, 0, 2)).reshape(local_len, width).astype(jnp.bfloat16)

    row_table = jnp.take(block_mask, positions // BLOCK, axis=0)
    own_block = (positions // BLOCK)[:, None] == (positions // BLOCK)[None, :]
    noisy_state = attend(start_state(heads, local_len), q_noisy, k_noisy, v_noisy, own_block)
    states = (start_state(heads, local_len), noisy_state)
    piece = lax.all_gather(key_values, "ctx", axis=1, tiled=True)
    count = piece.shape[1]
    visible = jnp.repeat(row_table, BLOCK, axis=1)
    keys = piece[0].reshape(count, heads, HEAD_DIM)
    values = piece[1].reshape(count, heads, HEAD_DIM)
    states = (
        attend(states[0], q_clean, keys, values, visible % 2 == 1),
        attend(states[1], q_noisy, keys, values, visible // 2 == 1),
    )
    attended = jnp.stack([finish(states[0]), finish(states[1])])
    model_width = w_out.shape[1]
    piece = attended
    summed = lax.psum_scatter(
        jnp.einsum("sqc,cd->qsd", piece, w_out, preferred_element_type=jnp.float32)
        .reshape(local_len // lax.axis_size("tp") * lax.axis_size("tp"), 2 * model_width)
        .astype(jnp.bfloat16),
        "tp",
        scatter_dimension=0,
        tiled=True,
    ).astype(jnp.float32)
    result = summed.reshape(summed.shape[0], 2, model_width)
    return (result[:, 0].astype(jnp.bfloat16), result[:, 1].astype(jnp.bfloat16))

LOG2E = 1.4426950408889634
MESH = pl.DeviceIdType.MESH


def layer_kernel(
    n_chips,
    x_ref, flag_ref, mask_ref, gain_ref, vis_ref, table_hbm, wq_hbm, wk_hbm, wv_hbm, wo_hbm,
    clean_ref, noisy_ref,
    w_s, wo_s, table, lhs0, lhs1, flag0, flag1, mproj, nb, sendq, sendkv, recvq, recvkv, kall, vall, bias,
    oown, lown, obuf, lbuf, oin, lin, att, psend, precv, pown,
    wsem, wosem, tsem, xs, xr, ss, sr, cs, cr, qs, qr, ls, lc, lq, fs, fr, os_, or_, es, er, ol, el, ps, pr,
):
    ctx = lax.axis_index("ctx")
    tp = lax.axis_index("tp")
    chip = ctx // 2
    core = ctx % 2
    rows = x_ref.shape[0]
    length = 2 * rows
    pairs = n_chips // 2
    hd = HEAD_DIM
    seq = 2 * n_chips * length
    per = length // BLOCK
    my_z = chip // 2
    w_hbm = (wq_hbm, wk_hbm, wv_hbm)
    twin = {"tp": 1 - tp}
    sibling = {"ctx": 2 * chip + 1 - core}

    def pair_at(i):
        return (my_z + 2 + i) % pairs

    def w_copy(kind, i):
        cols = pl.ds(pl.multiple_of(pair_at(i) * 2 * hd, 2 * hd), 2 * hd)
        return pltpu.make_async_copy(w_hbm[kind].at[:, cols], w_s.at[kind, :, cols], wsem.at[i, kind])

    def half_rows(half):
        which = tp if half == 0 else 1 - tp
        return pl.ds(pl.multiple_of(which * rows, rows), rows)

    table_copy = pltpu.make_async_copy(table_hbm.at[:, pl.ds(pl.multiple_of(ctx * length, length), length)], table, tsem)
    table_copy.start()
    for i in range(pairs):
        for kind in range(3):
            w_copy(kind, i).start()
    wo_copy = pltpu.make_async_copy(wo_hbm, wo_s, wosem)
    wo_copy.start()

    barrier = pltpu.get_barrier_semaphore()
    pl.semaphore_signal(barrier, inc=1, device_id=twin, device_id_type=MESH)
    pl.semaphore_signal(barrier, inc=1, device_id=sibling, device_id_type=MESH)
    for d in range(1, n_chips):
        peer = (chip + d) % n_chips
        pl.semaphore_signal(barrier, inc=1, device_id={"ctx": 2 * peer + core}, device_id_type=MESH)

    gain = gain_ref[...].reshape(1, x_ref.shape[1]).astype(jnp.float32)

    def norm(values):
        wide = values.astype(jnp.float32)
        factor = lax.rsqrt(jnp.mean(wide * wide, axis=-1, keepdims=True) + EPSILON)
        return (wide * factor * gain).astype(jnp.bfloat16)

    lhs0[0:rows, :] = norm(x_ref[...])
    lhs0[rows:rows + 16, :] = jnp.broadcast_to(norm(mask_ref[...].reshape(1, x_ref.shape[1])), (16, lhs0.shape[1]))
    flag0[...] = jnp.transpose(jnp.broadcast_to(flag_ref[...].astype(jnp.float32).reshape(1, rows), (hd, rows)))

    pl.semaphore_wait(barrier, n_chips + 1)

    def x_copy():
        return pltpu.make_async_remote_copy(
            src_ref=lhs0.at[pl.ds(0, rows)], dst_ref=lhs1, send_sem=xs.at[0], recv_sem=xr.at[0],
            device_id=twin, device_id_type=MESH)

    def flag_copy():
        return pltpu.make_async_remote_copy(
            src_ref=flag0, dst_ref=flag1, send_sem=xs.at[1], recv_sem=xr.at[1],
            device_id=twin, device_id_type=MESH)

    flag_copy().start()
    x_copy().start()

    def kv_copy(head, slot, half):
        where = half_rows(half)
        return pltpu.make_async_remote_copy(
            src_ref=sendkv.at[head, where], dst_ref=recvkv.at[slot, where],
            send_sem=ss.at[head, half], recv_sem=sr.at[slot, half],
            device_id={"ctx": 2 * head + core}, device_id_type=MESH)

    def clean_copy(head, slot, half):
        where = half_rows(half)
        return pltpu.make_async_remote_copy(
            src_ref=sendq.at[0, head, where], dst_ref=recvq.at[0, slot, where],
            send_sem=cs.at[head, half], recv_sem=cr.at[slot, half],
            device_id={"ctx": 2 * head + core}, device_id_type=MESH)

    def noisy_copy(head, slot):
        return pltpu.make_async_remote_copy(
            src_ref=sendq.at[1, head], dst_ref=recvq.at[1, slot], send_sem=qs.at[head], recv_sem=qr.at[slot],
            device_id={"ctx": 2 * head + core}, device_id_type=MESH)

    def kv_here(half):
        where = half_rows(half)
        return pltpu.make_async_copy(sendkv.at[chip, where], recvkv.at[chip, where], ls.at[half])

    def clean_here(half):
        where = half_rows(half)
        return pltpu.make_async_copy(sendq.at[0, chip, where], recvq.at[0, chip, where], lc.at[half])

    def noisy_here():
        return pltpu.make_async_copy(sendq.at[1, chip], recvq.at[1, chip], lq)

    key_at = lax.broadcasted_iota(jnp.int32, (vis_ref.shape[1], seq), 1)
    side = (key_at % (2 * length)) // length
    key_ctx = 2 * (key_at // (2 * length)) + jnp.where(side == 0, core, 1 - core)
    key_block = key_ctx * per + (key_at % length) // BLOCK
    spread = (lax.broadcasted_iota(jnp.int32, key_at.shape, 0) == key_block).astype(jnp.float32).astype(jnp.bfloat16)
    for copy in range(2):
        seen = ((vis_ref[...] >> copy) & 1).astype(jnp.float32).astype(jnp.bfloat16)
        shown = (jnp.dot(seen, spread, preferred_element_type=jnp.float32) - 1.0) * 1e30
        for c in range(2 * n_chips):
            bias[c, copy] = shown[c * per:(c + 1) * per]

    table_copy.wait()
    for half in range(2):
        if half == 1:
            flag_copy().wait_recv()
            x_copy().wait_recv()
        where = half_rows(half)

        def project(i, carry):
            pair = pair_at(i)
            cols = pl.ds(pl.multiple_of(pair * 2 * hd, 2 * hd), 2 * hd)
            if half == 0:
                for kind in range(3):
                    w_copy(kind, i).wait()
            flags = (flag0 if half == 0 else flag1)[...]
            cosine = table[0, where]
            sine = table[1, where]
            for kind in (1, 2, 0):
                left = (lhs0 if half == 0 else lhs1)[...]
                result = jnp.dot(left, w_s[kind, :, cols], preferred_element_type=jnp.float32)
                if half == 0:
                    mproj[kind, :, cols] = result[rows:rows + 8]
                    masked = result[rows:rows + 1]
                else:
                    masked = mproj[kind, :, cols][0:1]
                clean2 = result[0:rows]
                for k in range(2):
                    head = 2 * pair + k
                    clean = clean2[:, k * hd:(k + 1) * hd]
                    noisy = jnp.where(flags == 1.0, masked[:, k * hd:(k + 1) * hd], clean)
                    if kind < 2:
                        clean = clean * cosine + pltpu.roll(clean, hd // 2, 1) * sine
                        noisy = noisy * cosine + pltpu.roll(noisy, hd // 2, 1) * sine
                    clean = clean.astype(jnp.bfloat16)
                    noisy = noisy.astype(jnp.bfloat16)
                    if kind == 0:
                        sendq[0, head, where, :] = clean
                        sendq[1, head, where, :] = noisy
                    else:
                        nb[kind - 1, head, where, :] = noisy
                        sendkv[head, where, (kind - 1) * hd:kind * hd] = clean
                if kind != 1:
                    for k in range(2):
                        head = 2 * pair + k

                        @pl.when(head != chip)
                        def _():
                            (clean_copy if kind == 0 else kv_copy)(head, chip, half).start()

                        @pl.when(head == chip)
                        def _():
                            (clean_here if kind == 0 else kv_here)(half).start()
            return carry

        lax.fori_loop(0, pairs, project, 0)

    for d in range(1, n_chips):
        noisy_copy((chip + d) % n_chips, chip).start()
    noisy_here().start()

    scale = LOG2E * hd ** -0.5
    own = (lax.broadcasted_iota(jnp.int32, (length, length), 0) // BLOCK
           == lax.broadcasted_iota(jnp.int32, (length, length), 1) // BLOCK)

    def dot_t(a, b):
        return lax.dot_general(a, b, (((1,), (1,)), ((), ())), preferred_element_type=jnp.float32)

    for head in range(n_chips):
        scores = jnp.where(own, dot_t(sendq[1, head], nb[0, head]) * scale, NEG_FILL)
        peak = jnp.max(scores, axis=-1, keepdims=True)
        weights = jnp.exp2(scores - peak)
        total = jnp.sum(weights, axis=-1, keepdims=True)
        oown[head] = jnp.dot(weights.astype(jnp.bfloat16), nb[1, head], preferred_element_type=jnp.float32) / total
        lown[head] = jnp.broadcast_to(peak + jnp.log(total) * LOG2E, (length, hd))

    def share(p, kind):
        return pltpu.make_async_remote_copy(
            src_ref=recvkv.at[p, :, pl.ds(kind * hd, hd)],
            dst_ref=(kall, vall)[kind].at[p, pl.ds(length, length)],
            send_sem=fs.at[p, kind], recv_sem=fr.at[p, kind],
            device_id=sibling, device_id_type=MESH)

    def back(p, copy, slot):
        return pltpu.make_async_remote_copy(
            src_ref=obuf.at[copy, p], dst_ref=oin.at[copy, slot], send_sem=os_.at[copy, p], recv_sem=or_.at[copy, slot],
            device_id={"ctx": 2 * p + core}, device_id_type=MESH)

    def level_back(p, slot):
        return pltpu.make_async_remote_copy(
            src_ref=lbuf.at[p], dst_ref=lin.at[slot], send_sem=es.at[p], recv_sem=er.at[slot],
            device_id={"ctx": 2 * p + core}, device_id_type=MESH)

    def back_here(copy):
        return pltpu.make_async_copy(obuf.at[copy, chip], oin.at[copy, chip], ol.at[copy])

    def level_here():
        return pltpu.make_async_copy(lbuf.at[chip], lin.at[chip], el)

    for p in range(n_chips):
        for half in range(2):
            @pl.when(chip != p)
            def _():
                kv_copy(p, p, half).wait_recv()

            @pl.when(chip == p)
            def _():
                kv_here(half).wait()
        for kind in range(2):
            share(p, kind).start()
        kall[p, 0:length, :] = recvkv[p, :, 0:hd]
        vall[p, 0:length, :] = recvkv[p, :, hd:2 * hd]
    for p in range(n_chips):
        for kind in range(2):
            share(p, kind).wait_recv()

    chunks = psend.shape[1]
    width = psend.shape[3]

    def term_copy(copy, j):
        return pltpu.make_async_remote_copy(
            src_ref=psend.at[copy, j], dst_ref=precv.at[copy, j], send_sem=ps.at[copy, j], recv_sem=pr.at[copy, j],
            device_id=twin, device_id_type=MESH)

    def out_cols(j):
        return pl.ds(pl.multiple_of(j * width, width), width)

    def project_out(copy):
        mine = half_rows(0)
        theirs = half_rows(1)
        for head in range(n_chips):
            @pl.when(chip != head)
            def _():
                back(head, copy, head).wait_recv()

            @pl.when(chip == head)
            def _():
                back_here(copy).wait()
            if copy == 1:
                @pl.when(chip != head)
                def _():
                    level_back(head, head).wait_recv()

                @pl.when(chip == head)
                def _():
                    level_here().wait()
                away = jnp.transpose(jnp.broadcast_to(lin[head][0:1], (length, hd)))
                home = lown[head]
                top = jnp.maximum(away, home)
                w_away = jnp.exp2(away - top)
                w_home = jnp.exp2(home - top)
                noisy = oin[1, head].astype(jnp.float32)
                noisy = (noisy * w_away + oown[head] * w_home) / (w_away + w_home)
                oin[1, head] = noisy.astype(jnp.bfloat16)
            cols = slice(head * hd, (head + 1) * hd)
            att[copy, 0:rows, cols] = oin[copy, head, theirs, :]
            att[copy, rows:length, cols] = oin[copy, head, mine, :]

        def term(j, carry):
            both = jnp.dot(att[copy], wo_s[:, out_cols(j)], preferred_element_type=jnp.float32).astype(jnp.bfloat16)
            psend[copy, j] = both[0:rows]
            pown[copy, j] = both[rows:length]
            term_copy(copy, j).start()
            return carry

        lax.fori_loop(0, chunks, term, 0)

    def attend_step(step, carry):
        copy = step // n_chips
        p = (chip + step) % n_chips

        @pl.when((copy == 0) & (chip != p))
        def _():
            for half in range(2):
                clean_copy(p, p, half).wait_recv()

        @pl.when((copy == 0) & (chip == p))
        def _():
            for half in range(2):
                clean_here(half).wait()

        @pl.when((copy == 1) & (chip != p))
        def _():
            noisy_copy(p, p).wait_recv()

        @pl.when((copy == 1) & (chip == p))
        def _():
            noisy_here().wait()

        for k in range(n_chips):
            @pl.when(p == k)
            def _():
                count = (k + 1) * 2 * length
                keys = kall[0:k + 1].reshape(count, hd)
                values = vall[0:k + 1].reshape(count, hd)
                shown = bias[2 * k + core, copy][:, 0:count]
                queries = recvq[copy, k]
                extra = jnp.concatenate(
                    [jnp.broadcast_to(shown[b:b + 1], (BLOCK, count)) for b in range(per)], axis=0)
                scores = dot_t(queries, keys) * scale + extra
                peak = jnp.max(scores, axis=-1, keepdims=True)
                weights = jnp.exp2(scores - peak)
                total = jnp.sum(weights, axis=-1, keepdims=True)
                result = jnp.dot(weights.astype(jnp.bfloat16), values, preferred_element_type=jnp.float32) / total
                obuf[copy, k] = result.astype(jnp.bfloat16)

                @pl.when(copy == 1)
                def _():
                    level = jnp.broadcast_to(peak + jnp.log(total) * LOG2E, (length, hd))
                    lbuf[k] = jnp.transpose(level)[0:8]

        @pl.when(chip != p)
        def _():
            back(p, copy, chip).start()

        @pl.when(chip == p)
        def _():
            back_here(copy).start()

        @pl.when((copy == 1) & (chip != p))
        def _():
            level_back(p, chip).start()

        @pl.when((copy == 1) & (chip == p))
        def _():
            level_here().start()

        @pl.when(step == n_chips + n_chips // 2 - 1)
        def _():
            wo_copy.wait()
            project_out(0)
        return carry

    lax.fori_loop(0, 2 * n_chips, attend_step, 0)
    project_out(1)

    for copy, out_ref in ((0, clean_ref), (1, noisy_ref)):
        def total_of(j, carry):
            term_copy(copy, j).wait_recv()
            out_ref[:, out_cols(j)] = pown[copy, j].astype(jnp.float32) + precv[copy, j].astype(jnp.float32)
            return carry

        lax.fori_loop(0, chunks, total_of, 0)

    flag_copy().wait_send()
    x_copy().wait_send()
    for p in range(n_chips):
        for kind in range(2):
            share(p, kind).wait_send()

        @pl.when(chip != p)
        def _():
            for half in range(2):
                kv_copy(p, chip, half).wait_send()
                clean_copy(p, chip, half).wait_send()
            noisy_copy(p, chip).wait_send()
            for copy in range(2):
                back(p, copy, chip).wait_send()
            level_back(p, chip).wait_send()
    for copy in range(2):
        for j in range(chunks):
            term_copy(copy, j).wait_send()


def rotary_table(length):
    indices = np.arange(HEAD_DIM // 2).astype(np.float32)
    freqs = (ROPE_BASE ** (-2.0 * indices.astype(np.float64) / HEAD_DIM)).astype(np.float32)
    angles = (np.arange(length, dtype=np.float32)[:, None] * freqs[None, :]).astype(np.float64)
    cosine = np.cos(angles).astype(np.float32)
    sine = np.sin(angles).astype(np.float32)
    return np.stack([np.concatenate([cosine, cosine], axis=1), np.concatenate([-sine, sine], axis=1)])


def local_kernel(
    tokens_clean, noise_mask, mask_embed, norm_gain, w_query, w_key, w_value, w_out, block_mask
):
    rows, model = tokens_clean.shape
    length = 2 * rows
    width = w_query.shape[1]
    n_chips = width // HEAD_DIM
    hd = HEAD_DIM
    seq = 2 * n_chips * length
    per = length // BLOCK
    bf, f32 = jnp.bfloat16, jnp.float32
    chunks = 8
    part = model // chunks
    dma = pltpu.SemaphoreType.DMA
    vmem = pl.BlockSpec(memory_space=pltpu.VMEM)
    hbm = pl.BlockSpec(memory_space=pl.ANY)
    clean, noisy = pl.pallas_call(
        functools.partial(layer_kernel, n_chips),
        out_shape=(jax.ShapeDtypeStruct((rows, model), f32), jax.ShapeDtypeStruct((rows, model), f32)),
        in_specs=[vmem] * 5 + [hbm] * 5,
        out_specs=(vmem, vmem),
        scratch_shapes=[
            pltpu.VMEM((3, model, width), bf),
            pltpu.VMEM((width, model), bf),
            pltpu.VMEM((2, length, hd), f32),
            pltpu.VMEM((rows + 16, model), bf),
            pltpu.VMEM((rows, model), bf),
            pltpu.VMEM((rows, hd), f32),
            pltpu.VMEM((rows, hd), f32),
            pltpu.VMEM((3, 8, width), f32),
            pltpu.VMEM((2, n_chips, length, hd), bf),
            pltpu.VMEM((2, n_chips, length, hd), bf),
            pltpu.VMEM((n_chips, length, 2 * hd), bf),
            pltpu.VMEM((2, n_chips, length, hd), bf),
            pltpu.VMEM((n_chips, length, 2 * hd), bf),
            pltpu.VMEM((n_chips, 2 * length, hd), bf),
            pltpu.VMEM((n_chips, 2 * length, hd), bf),
            pltpu.VMEM((2 * n_chips, 2, per, seq), f32),
            pltpu.VMEM((n_chips, length, hd), f32),
            pltpu.VMEM((n_chips, length, hd), f32),
            pltpu.VMEM((2, n_chips, length, hd), bf),
            pltpu.VMEM((n_chips, 8, hd), f32),
            pltpu.VMEM((2, n_chips, length, hd), bf),
            pltpu.VMEM((n_chips, 8, hd), f32),
            pltpu.VMEM((2, length, width), bf),
            pltpu.VMEM((2, chunks, rows, part), bf),
            pltpu.VMEM((2, chunks, rows, part), bf),
            pltpu.VMEM((2, chunks, rows, part), bf),
            dma((n_chips // 2, 3)),
            dma,
            dma,
            dma((2,)),
            dma((2,)),
            dma((n_chips, 2)),
            dma((n_chips, 2)),
            dma((n_chips, 2)),
            dma((n_chips, 2)),
            dma((n_chips,)),
            dma((n_chips,)),
            dma((2,)),
            dma((2,)),
            dma,
            dma((n_chips, 2)),
            dma((n_chips, 2)),
            dma((2, n_chips)),
            dma((2, n_chips)),
            dma((n_chips,)),
            dma((n_chips,)),
            dma((2,)),
            dma,
            dma((2, chunks)),
            dma((2, chunks)),
        ],
        compiler_params=pltpu.CompilerParams(
            collective_id=0, has_side_effects=True, vmem_limit_bytes=60 * 1024 * 1024),
        cost_estimate=pl.CostEstimate(flops=6 * 10**9, bytes_accessed=34 * 2**20, transcendentals=3 * 10**6),
    )(tokens_clean, noise_mask, mask_embed, norm_gain, block_mask, jnp.asarray(rotary_table(seq)),
      w_query, w_key, w_value, w_out)
    return (clean.astype(bf), noisy.astype(bf))


def fits(mesh, tokens_clean, w_query):
    n_ctx, n_tp = mesh.shape["ctx"], mesh.shape["tp"]
    heads = w_query.shape[1] // n_tp // HEAD_DIM
    tokens = tokens_clean.shape[0] // n_ctx
    return n_tp == 2 and n_ctx == 2 * heads and heads % 4 == 0 and tokens == HEAD_DIM


def solution(mesh):
    specs = dict(
        mesh=mesh,
        in_specs=(
            P(("ctx", "tp"), None),
            P(("ctx", "tp")),
            P(),
            P(),
            P(None, "tp"),
            P(None, "tp"),
            P(None, "tp"),
            P("tp", None),
            P(),
        ),
        out_specs=(P(("ctx", "tp"), None), P(("ctx", "tp"), None)),
        check_vma=False,
    )

    def layer(tokens_clean, noise_mask, mask_embed, norm_gain, w_query, w_key, w_value, w_out, block_mask):
        body = local_kernel if fits(mesh, tokens_clean, w_query) else local
        return jax.shard_map(body, **specs)(
            tokens_clean, noise_mask, mask_embed, norm_gain, w_query, w_key, w_value, w_out, block_mask)

    return layer
```

```python
import functools

import jax
import jax.numpy as jnp
import numpy as np
from jax import lax
from jax.experimental import pallas as pl
from jax.experimental.pallas import tpu as pltpu
from jax.sharding import PartitionSpec as P

HEAD_DIM = 128
BLOCK = 32


ROPE_BASE = 500000.0
EPSILON = 1e-05
NEG_FILL = -1e30


def rms_rows(values, gain):
    wide = values.astype(jnp.float32)
    factor = lax.rsqrt(jnp.mean(wide * wide, axis=-1, keepdims=True) + EPSILON)
    return (wide * factor * gain.astype(jnp.float32)).astype(jnp.bfloat16)


def rotate(values, positions):
    half_dim = values.shape[-1] // 2
    indices = jnp.arange(half_dim).astype(jnp.float32)
    freqs = ROPE_BASE ** (-2.0 * indices / values.shape[-1])
    angles = positions.astype(jnp.float32)[:, None] * freqs[None, :]
    cosine = jnp.cos(angles)[:, None, :]
    sine = jnp.sin(angles)[:, None, :]
    lower = values[..., :half_dim]
    upper = values[..., half_dim:]
    return jnp.concatenate([lower * cosine - upper * sine, upper * cosine + lower * sine], axis=-1)


def start_state(heads, length):
    return (
        jnp.full((heads, length), NEG_FILL, jnp.float32),
        jnp.zeros((heads, length), jnp.float32),
        jnp.zeros((heads, length, HEAD_DIM), jnp.float32),
    )


def attend(state, queries, keys, values, visible):
    peak_old, total_old, weighted_old = state
    scores = jnp.einsum(
        "qhd,khd->hqk", queries, keys, preferred_element_type=jnp.float32
    ) * HEAD_DIM ** (-0.5)
    scores = jnp.where(visible[None], scores, NEG_FILL)
    peak_new = jnp.maximum(peak_old, jnp.max(scores, axis=-1))
    weights = jnp.where(visible[None], jnp.exp(scores - peak_new[..., None]), 0.0)
    factor = jnp.exp(peak_old - peak_new)
    total_new = total_old * factor + jnp.sum(weights, axis=-1)
    weighted_new = weighted_old * factor[..., None] + jnp.einsum(
        "hqk,khd->hqd", weights.astype(jnp.bfloat16), values, preferred_element_type=jnp.float32
    )
    return (peak_new, total_new, weighted_new)


def local(
    tokens_clean, noise_mask, mask_embed, norm_gain, w_query, w_key, w_value, w_out, block_mask
):
    normed = rms_rows(tokens_clean, norm_gain)
    mask_row = rms_rows(mask_embed[None, :], norm_gain)
    gathered, noise_flags = (
        lax.all_gather(normed, "tp", axis=0, tiled=True),
        lax.all_gather(noise_mask, "tp", axis=0, tiled=True),
    )
    local_len = gathered.shape[0]
    width = w_query.shape[1]
    heads = width // HEAD_DIM
    first_row = lax.axis_index("ctx") * local_len
    positions = first_row + jnp.arange(local_len, dtype=jnp.int32)
    noisy_rows = (noise_flags == 1)[:, None]

    def project(weight, rotary):
        clean = jnp.dot(gathered, weight, preferred_element_type=jnp.float32)
        masked = jnp.dot(mask_row, weight, preferred_element_type=jnp.float32)
        noisy = jnp.where(noisy_rows, masked, clean)
        clean = clean.reshape(local_len, heads, HEAD_DIM)
        noisy = noisy.reshape(local_len, heads, HEAD_DIM)
        if rotary:
            clean = rotate(clean, positions)
            noisy = rotate(noisy, positions)
        return (clean.astype(jnp.bfloat16), noisy.astype(jnp.bfloat16))

    q_clean, q_noisy = project(w_query, True)
    k_clean, k_noisy = project(w_key, True)
    v_clean, v_noisy = project(w_value, False)
    key_values = jnp.stack([k_clean.reshape(local_len, width), v_clean.reshape(local_len, width)])

    def finish(state):
        weighted = state[2] / state[1][..., None]
        return jnp.transpose(weighted, (1, 0, 2)).reshape(local_len, width).astype(jnp.bfloat16)

    row_table = jnp.take(block_mask, positions // BLOCK, axis=0)
    own_block = (positions // BLOCK)[:, None] == (positions // BLOCK)[None, :]
    noisy_state = attend(start_state(heads, local_len), q_noisy, k_noisy, v_noisy, own_block)
    states = (start_state(heads, local_len), noisy_state)
    piece = lax.all_gather(key_values, "ctx", axis=1, tiled=True)
    count = piece.shape[1]
    visible = jnp.repeat(row_table, BLOCK, axis=1)
    keys = piece[0].reshape(count, heads, HEAD_DIM)
    values = piece[1].reshape(count, heads, HEAD_DIM)
    states = (
        attend(states[0], q_clean, keys, values, visible % 2 == 1),
        attend(states[1], q_noisy, keys, values, visible // 2 == 1),
    )
    attended = jnp.stack([finish(states[0]), finish(states[1])])
    model_width = w_out.shape[1]
    piece = attended
    summed = lax.psum_scatter(
        jnp.einsum("sqc,cd->qsd", piece, w_out, preferred_element_type=jnp.float32)
        .reshape(local_len // lax.axis_size("tp") * lax.axis_size("tp"), 2 * model_width)
        .astype(jnp.bfloat16),
        "tp",
        scatter_dimension=0,
        tiled=True,
    ).astype(jnp.float32)
    result = summed.reshape(summed.shape[0], 2, model_width)
    return (result[:, 0].astype(jnp.bfloat16), result[:, 1].astype(jnp.bfloat16))

LOG2E = 1.4426950408889634
MESH = pl.DeviceIdType.MESH


def layer_kernel(
    n_chips,
    x_ref, flag_ref, mask_ref, gain_ref, vis_ref, table_hbm, wq_hbm, wk_hbm, wv_hbm, wo_hbm,
    out_ref,
    w_s, wo_s, table, lhs0, lhs1, row0, row1, flags, rowall, rowin, mproj, nb, sendq, sendkv, recvq, recvkv, kall, vall, bias,
    oown, lown, obuf, lbuf, oin, lin, att, psend, precv, pown,
    wsem, wosem, tsem, xs, xr, ss, sr, cs, cr, gs, gr, ls, lc, lg, fs, fr, os_, or_, es, er, ol, el, ps, pr,
):
    ctx = lax.axis_index("ctx")
    tp = lax.axis_index("tp")
    chip = ctx // 2
    core = ctx % 2
    rows = x_ref.shape[0]
    length = 2 * rows
    pairs = n_chips // 2
    hd = HEAD_DIM
    seq = 2 * n_chips * length
    per = length // BLOCK
    my_z = chip // 2
    w_hbm = (wq_hbm, wk_hbm, wv_hbm)
    twin = {"tp": 1 - tp}
    sibling = {"ctx": 2 * chip + 1 - core}

    def pair_at(i):
        return (my_z + 2 + i) % pairs

    def w_copy(kind, i):
        cols = pl.ds(pl.multiple_of(pair_at(i) * 2 * hd, 2 * hd), 2 * hd)
        return pltpu.make_async_copy(w_hbm[kind].at[:, cols], w_s.at[kind, :, cols], wsem.at[i, kind])

    def half_rows(half):
        which = tp if half == 0 else 1 - tp
        return pl.ds(pl.multiple_of(which * rows, rows), rows)

    table_copy = pltpu.make_async_copy(table_hbm, table, tsem)
    for i in range(pairs):
        for kind in (1, 2, 0):
            w_copy(kind, i).start()
        if i == 0:
            table_copy.start()
    wo_copy = pltpu.make_async_copy(wo_hbm, wo_s, wosem)
    wo_copy.start()

    barrier = pltpu.get_barrier_semaphore()
    pl.semaphore_signal(barrier, inc=1, device_id=twin, device_id_type=MESH)
    pl.semaphore_signal(barrier, inc=1, device_id=sibling, device_id_type=MESH)
    for d in range(1, n_chips):
        peer = (chip + d) % n_chips
        pl.semaphore_signal(barrier, inc=1, device_id={"ctx": 2 * peer + core}, device_id_type=MESH)

    gain = gain_ref[...].reshape(1, x_ref.shape[1]).astype(jnp.float32)

    def norm(values):
        wide = values.astype(jnp.float32)
        factor = lax.rsqrt(jnp.mean(wide * wide, axis=-1, keepdims=True) + EPSILON)
        return (wide * factor * gain).astype(jnp.bfloat16)

    lhs0[0:rows, :] = norm(x_ref[...])
    lhs0[rows:rows + 16, :] = jnp.broadcast_to(norm(mask_ref[...].reshape(1, x_ref.shape[1])), (16, lhs0.shape[1]))
    flag_row = flag_ref[...].astype(jnp.float32).reshape(1, rows)
    row0[...] = jnp.broadcast_to(jnp.concatenate([flag_row, flag_row], axis=1), row0.shape)

    pl.semaphore_wait(barrier, n_chips + 1)

    def x_copy():
        return pltpu.make_async_remote_copy(
            src_ref=lhs0.at[pl.ds(0, rows)], dst_ref=lhs1, send_sem=xs.at[0], recv_sem=xr.at[0],
            device_id=twin, device_id_type=MESH)

    def flag_copy():
        return pltpu.make_async_remote_copy(
            src_ref=row0, dst_ref=row1, send_sem=xs.at[1], recv_sem=xr.at[1],
            device_id=twin, device_id_type=MESH)

    flag_copy().start()
    x_copy().start()

    def kv_copy(head, slot, half):
        where = half_rows(half)
        return pltpu.make_async_remote_copy(
            src_ref=sendkv.at[head, where], dst_ref=recvkv.at[slot, where],
            send_sem=ss.at[head, half], recv_sem=sr.at[slot, half],
            device_id={"ctx": 2 * head + core}, device_id_type=MESH)

    def clean_copy(head, slot, half):
        where = half_rows(half)
        return pltpu.make_async_remote_copy(
            src_ref=sendq.at[0, head, where], dst_ref=recvq.at[0, slot, where],
            send_sem=cs.at[head, half], recv_sem=cr.at[slot, half],
            device_id={"ctx": 2 * head + core}, device_id_type=MESH)

    def row_copy(head, slot):
        return pltpu.make_async_remote_copy(
            src_ref=rowall, dst_ref=rowin.at[slot], send_sem=gs.at[head], recv_sem=gr.at[slot],
            device_id={"ctx": 2 * head + core}, device_id_type=MESH)

    def kv_here(half):
        where = half_rows(half)
        return pltpu.make_async_copy(sendkv.at[chip, where], recvkv.at[chip, where], ls.at[half])

    def clean_here(half):
        where = half_rows(half)
        return pltpu.make_async_copy(sendq.at[0, chip, where], recvq.at[0, chip, where], lc.at[half])

    def row_here():
        return pltpu.make_async_copy(rowall, rowin.at[chip], lg)

    def column(row):
        return jnp.transpose(jnp.broadcast_to(row, (length, length)))

    flag_copy().wait_recv()
    lane = lax.broadcasted_iota(jnp.int32, row0.shape, 1)
    rowall[...] = jnp.where(lane // rows == tp, row0[...], row1[...])
    for d in range(1, n_chips):
        row_copy((chip + d) % n_chips, chip).start()
    row_here().start()
    flags[...] = column(rowall[0:1])

    table_copy.wait()
    for half in range(2):
        if half == 1:
            x_copy().wait_recv()
        where = half_rows(half)

        def project(i, carry):
            pair = pair_at(i)
            cols = pl.ds(pl.multiple_of(pair * 2 * hd, 2 * hd), 2 * hd)
            if half == 0:
                for kind in range(3):
                    w_copy(kind, i).wait()
            flag = flags[where]
            token_rows = pl.ds(pl.multiple_of(ctx * length + (tp if half == 0 else 1 - tp) * rows, rows), rows)
            cosine = table[0, token_rows]
            sine = table[1, token_rows]
            for kind in (1, 2, 0):
                left = (lhs0 if half == 0 else lhs1)[...]
                result = jnp.dot(left, w_s[kind, :, cols], preferred_element_type=jnp.float32)
                if half == 0:
                    mproj[kind, :, cols] = result[rows:rows + 8]
                    masked = result[rows:rows + 1]
                else:
                    masked = mproj[kind, :, cols][0:1]
                clean2 = result[0:rows]
                for k in range(2):
                    head = 2 * pair + k
                    clean = clean2[:, k * hd:(k + 1) * hd]
                    noisy = jnp.where(flag == 1.0, masked[:, k * hd:(k + 1) * hd], clean)
                    if kind < 2:
                        clean = clean * cosine + pltpu.roll(clean, hd // 2, 1) * sine
                        noisy = noisy * cosine + pltpu.roll(noisy, hd // 2, 1) * sine
                    clean = clean.astype(jnp.bfloat16)
                    noisy = noisy.astype(jnp.bfloat16)
                    if kind == 0:
                        sendq[0, head, where, :] = clean
                        sendq[1, head, where, :] = noisy
                    else:
                        nb[kind - 1, head, where, :] = noisy
                        sendkv[head, where, (kind - 1) * hd:kind * hd] = clean
                if kind != 1:
                    for k in range(2):
                        head = 2 * pair + k

                        @pl.when(head != chip)
                        def _():
                            (clean_copy if kind == 0 else kv_copy)(head, chip, half).start()

                        @pl.when(head == chip)
                        def _():
                            (clean_here if kind == 0 else kv_here)(half).start()
            return carry

        lax.fori_loop(0, pairs, project, 0)

    key_at = lax.broadcasted_iota(jnp.int32, (vis_ref.shape[1], seq), 1)
    side = (key_at % (2 * length)) // length
    key_ctx = 2 * (key_at // (2 * length)) + jnp.where(side == 0, core, 1 - core)
    key_block = key_ctx * per + (key_at % length) // BLOCK
    spread = (lax.broadcasted_iota(jnp.int32, key_at.shape, 0) == key_block).astype(jnp.float32).astype(jnp.bfloat16)
    for copy in range(2):
        seen = ((vis_ref[...] >> copy) & 1).astype(jnp.float32).astype(jnp.bfloat16)
        shown = (jnp.dot(seen, spread, preferred_element_type=jnp.float32) - 1.0) * 1e30
        for c in range(2 * n_chips):
            bias[c, copy] = shown[c * per:(c + 1) * per]

    scale = LOG2E * hd ** -0.5
    own = (lax.broadcasted_iota(jnp.int32, (length, length), 0) // BLOCK
           == lax.broadcasted_iota(jnp.int32, (length, length), 1) // BLOCK)

    def dot_t(a, b):
        return lax.dot_general(a, b, (((1,), (1,)), ((), ())), preferred_element_type=jnp.float32)

    for head in range(n_chips):
        scores = jnp.where(own, dot_t(sendq[1, head], nb[0, head]) * scale, NEG_FILL)
        peak = jnp.max(scores, axis=-1, keepdims=True)
        weights = jnp.exp2(scores - peak)
        total = jnp.sum(weights, axis=-1, keepdims=True)
        oown[head] = jnp.dot(weights.astype(jnp.bfloat16), nb[1, head], preferred_element_type=jnp.float32) / total
        lown[head] = jnp.broadcast_to(peak + jnp.log(total) * LOG2E, (length, hd))

    def share(p, kind):
        return pltpu.make_async_remote_copy(
            src_ref=recvkv.at[p, :, pl.ds(kind * hd, hd)],
            dst_ref=(kall, vall)[kind].at[p, pl.ds(length, length)],
            send_sem=fs.at[p, kind], recv_sem=fr.at[p, kind],
            device_id=sibling, device_id_type=MESH)

    def back(p, copy, slot):
        return pltpu.make_async_remote_copy(
            src_ref=obuf.at[copy, p], dst_ref=oin.at[copy, slot], send_sem=os_.at[copy, p], recv_sem=or_.at[copy, slot],
            device_id={"ctx": 2 * p + core}, device_id_type=MESH)

    def level_back(p, slot):
        return pltpu.make_async_remote_copy(
            src_ref=lbuf.at[1, p], dst_ref=lin.at[slot], send_sem=es.at[p], recv_sem=er.at[slot],
            device_id={"ctx": 2 * p + core}, device_id_type=MESH)

    def back_here(copy):
        return pltpu.make_async_copy(obuf.at[copy, chip], oin.at[copy, chip], ol.at[copy])

    def level_here():
        return pltpu.make_async_copy(lbuf.at[1, chip], lin.at[chip], el)

    for p in range(n_chips):
        for half in range(2):
            @pl.when(chip != p)
            def _():
                kv_copy(p, p, half).wait_recv()

            @pl.when(chip == p)
            def _():
                kv_here(half).wait()
        for kind in range(2):
            share(p, kind).start()
        kall[p, 0:length, :] = recvkv[p, :, 0:hd]
        vall[p, 0:length, :] = recvkv[p, :, hd:2 * hd]
    for p in range(n_chips):
        for kind in range(2):
            share(p, kind).wait_recv()

    chunks = psend.shape[1]
    width = psend.shape[3]

    def term_copy(copy, j):
        return pltpu.make_async_remote_copy(
            src_ref=psend.at[copy, j], dst_ref=precv.at[copy, j], send_sem=ps.at[copy, j], recv_sem=pr.at[copy, j],
            device_id=twin, device_id_type=MESH)

    def out_cols(j):
        return pl.ds(pl.multiple_of(j * width, width), width)

    def project_out(copy):
        mine = half_rows(0)
        theirs = half_rows(1)
        for head in range(n_chips):
            @pl.when(chip != head)
            def _():
                back(head, copy, head).wait_recv()

            @pl.when(chip == head)
            def _():
                back_here(copy).wait()
            if copy == 1:
                @pl.when(chip != head)
                def _():
                    level_back(head, head).wait_recv()

                @pl.when(chip == head)
                def _():
                    level_here().wait()
                away = jnp.transpose(jnp.broadcast_to(lin[head][0:1], (length, hd)))
                home = lown[head]
                top = jnp.maximum(away, home)
                w_away = jnp.exp2(away - top)
                w_home = jnp.exp2(home - top)
                noisy = oin[1, head].astype(jnp.float32)
                noisy = (noisy * w_away + oown[head] * w_home) / (w_away + w_home)
                oin[1, head] = noisy.astype(jnp.bfloat16)
            cols = slice(head * hd, (head + 1) * hd)
            att[copy, 0:rows, cols] = oin[copy, head, theirs, :]
            att[copy, rows:length, cols] = oin[copy, head, mine, :]

        def term(j, carry):
            both = jnp.dot(att[copy], wo_s[:, out_cols(j)], preferred_element_type=jnp.float32).astype(jnp.bfloat16)
            psend[copy, j] = both[0:rows]
            pown[copy, j] = both[rows:length]
            term_copy(copy, j).start()
            return carry

        lax.fori_loop(0, chunks, term, 0)

    def attend_step(step, carry):
        copy = step // pairs
        low = (my_z + step) % pairs
        chosen = (low, n_chips - 1 - low)
        for p in chosen:
            @pl.when((copy == 0) & (chip != p))
            def _():
                for half in range(2):
                    clean_copy(p, p, half).wait_recv()
                row_copy(p, p).wait_recv()

            @pl.when((copy == 0) & (chip == p))
            def _():
                for half in range(2):
                    clean_here(half).wait()
                row_here().wait()

            @pl.when(copy == 1)
            def _():
                token_rows = pl.ds(pl.multiple_of((2 * p + core) * length, length), length)
                masked = jnp.broadcast_to(mproj[0, :, pl.ds(pl.multiple_of(chip * hd, hd), hd)][0:1], (length, hd))
                masked = masked * table[0, token_rows] + pltpu.roll(masked, hd // 2, 1) * table[1, token_rows]
                clean = recvq[0, p].astype(jnp.float32)
                recvq[1, p] = jnp.where(column(rowin[p][0:1]) == 1.0, masked, clean).astype(jnp.bfloat16)

        for k in range(pairs):
            @pl.when(low == k)
            def _():
                for q in (k, n_chips - 1 - k):
                    count = (q + 1) * 2 * length
                    keys = kall[0:q + 1].reshape(count, hd)
                    values = vall[0:q + 1].reshape(count, hd)
                    shown = bias[2 * q + core, copy][:, 0:count]
                    extra = jnp.concatenate(
                        [jnp.broadcast_to(shown[b:b + 1], (BLOCK, count)) for b in range(per)], axis=0)
                    scores = dot_t(recvq[copy, q], keys) * scale + extra
                    peak = jnp.max(scores, axis=-1, keepdims=True)
                    weights = jnp.exp2(scores - peak)
                    total = jnp.sum(weights, axis=-1, keepdims=True)
                    result = jnp.dot(weights.astype(jnp.bfloat16), values, preferred_element_type=jnp.float32) / total
                    obuf[copy, q] = result.astype(jnp.bfloat16)
                    level = jnp.broadcast_to(peak + jnp.log(total) * LOG2E, (length, hd))
                    lbuf[copy, q] = jnp.transpose(level)[0:8]

        for p in chosen:
            @pl.when(chip != p)
            def _():
                back(p, copy, chip).start()

            @pl.when(chip == p)
            def _():
                back_here(copy).start()

            @pl.when((copy == 1) & (chip != p))
            def _():
                level_back(p, chip).start()

            @pl.when((copy == 1) & (chip == p))
            def _():
                level_here().start()

        @pl.when(step == pairs + pairs // 2 - 1)
        def _():
            wo_copy.wait()
            project_out(0)
        return carry

    lax.fori_loop(0, 2 * pairs, attend_step, 0)
    project_out(1)

    for copy in range(2):
        def total_of(j, carry):
            term_copy(copy, j).wait_recv()
            summed = pown[copy, j].astype(jnp.float32) + precv[copy, j].astype(jnp.float32)
            out_ref[copy, :, out_cols(j)] = summed.astype(jnp.bfloat16)
            return carry

        lax.fori_loop(0, chunks, total_of, 0)

    flag_copy().wait_send()
    x_copy().wait_send()
    for p in range(n_chips):
        for kind in range(2):
            share(p, kind).wait_send()

        @pl.when(chip != p)
        def _():
            for half in range(2):
                kv_copy(p, chip, half).wait_send()
                clean_copy(p, chip, half).wait_send()
            row_copy(p, chip).wait_send()
            for copy in range(2):
                back(p, copy, chip).wait_send()
            level_back(p, chip).wait_send()
    for copy in range(2):
        for j in range(chunks):
            term_copy(copy, j).wait_send()


def place_kernel(both, clean, noisy, sems):
    half = clean.shape[0] // 2
    copies = [
        pltpu.make_async_copy(both.at[c, pl.ds(h * half, half)], out.at[pl.ds(h * half, half)], sems.at[c, h])
        for c, out in enumerate((clean, noisy)) for h in range(2)
    ]
    for copy in copies:
        copy.start()
    for copy in copies:
        copy.wait()


def rotary_table(length):
    indices = np.arange(HEAD_DIM // 2).astype(np.float32)
    freqs = (ROPE_BASE ** (-2.0 * indices.astype(np.float64) / HEAD_DIM)).astype(np.float32)
    angles = (np.arange(length, dtype=np.float32)[:, None] * freqs[None, :]).astype(np.float64)
    cosine = np.cos(angles).astype(np.float32)
    sine = np.sin(angles).astype(np.float32)
    return np.stack([np.concatenate([cosine, cosine], axis=1), np.concatenate([-sine, sine], axis=1)])


def local_kernel(
    tokens_clean, noise_mask, mask_embed, norm_gain, w_query, w_key, w_value, w_out, block_mask
):
    rows, model = tokens_clean.shape
    length = 2 * rows
    width = w_query.shape[1]
    n_chips = width // HEAD_DIM
    hd = HEAD_DIM
    seq = 2 * n_chips * length
    per = length // BLOCK
    bf, f32 = jnp.bfloat16, jnp.float32
    chunks = 8
    part = model // chunks
    dma = pltpu.SemaphoreType.DMA
    vmem = pl.BlockSpec(memory_space=pltpu.VMEM)
    hbm = pl.BlockSpec(memory_space=pl.ANY)
    both = pl.pallas_call(
        functools.partial(layer_kernel, n_chips),
        out_shape=jax.ShapeDtypeStruct((2, rows, model), bf),
        in_specs=[vmem] * 5 + [hbm] * 5,
        out_specs=vmem,
        scratch_shapes=[
            pltpu.VMEM((3, model, width), bf),
            pltpu.VMEM((width, model), bf),
            pltpu.VMEM((2, seq, hd), f32),
            pltpu.VMEM((rows + 16, model), bf),
            pltpu.VMEM((rows, model), bf),
            pltpu.VMEM((8, length), f32),
            pltpu.VMEM((8, length), f32),
            pltpu.VMEM((length, hd), f32),
            pltpu.VMEM((8, length), f32),
            pltpu.VMEM((n_chips, 8, length), f32),
            pltpu.VMEM((3, 8, width), f32),
            pltpu.VMEM((2, n_chips, length, hd), bf),
            pltpu.VMEM((2, n_chips, length, hd), bf),
            pltpu.VMEM((n_chips, length, 2 * hd), bf),
            pltpu.VMEM((2, n_chips, length, hd), bf),
            pltpu.VMEM((n_chips, length, 2 * hd), bf),
            pltpu.VMEM((n_chips, 2 * length, hd), bf),
            pltpu.VMEM((n_chips, 2 * length, hd), bf),
            pltpu.VMEM((2 * n_chips, 2, per, seq), f32),
            pltpu.VMEM((n_chips, length, hd), f32),
            pltpu.VMEM((n_chips, length, hd), f32),
            pltpu.VMEM((2, n_chips, length, hd), bf),
            pltpu.VMEM((2, n_chips, 8, hd), f32),
            pltpu.VMEM((2, n_chips, length, hd), bf),
            pltpu.VMEM((n_chips, 8, hd), f32),
            pltpu.VMEM((2, length, width), bf),
            pltpu.VMEM((2, chunks, rows, part), bf),
            pltpu.VMEM((2, chunks, rows, part), bf),
            pltpu.VMEM((2, chunks, rows, part), bf),
            dma((n_chips // 2, 3)),
            dma,
            dma,
            dma((2,)),
            dma((2,)),
            dma((n_chips, 2)),
            dma((n_chips, 2)),
            dma((n_chips, 2)),
            dma((n_chips, 2)),
            dma((n_chips,)),
            dma((n_chips,)),
            dma((2,)),
            dma((2,)),
            dma,
            dma((n_chips, 2)),
            dma((n_chips, 2)),
            dma((2, n_chips)),
            dma((2, n_chips)),
            dma((n_chips,)),
            dma((n_chips,)),
            dma((2,)),
            dma,
            dma((2, chunks)),
            dma((2, chunks)),
        ],
        compiler_params=pltpu.CompilerParams(
            collective_id=0, has_side_effects=True, vmem_limit_bytes=60 * 1024 * 1024),
        cost_estimate=pl.CostEstimate(flops=6 * 10**9, bytes_accessed=34 * 2**20, transcendentals=3 * 10**6),
    )(tokens_clean, noise_mask, mask_embed, norm_gain, block_mask, jnp.asarray(rotary_table(seq)),
      w_query, w_key, w_value, w_out)
    return pl.pallas_call(
        place_kernel,
        out_shape=(jax.ShapeDtypeStruct((rows, model), bf), jax.ShapeDtypeStruct((rows, model), bf)),
        in_specs=[hbm],
        out_specs=(hbm, hbm),
        scratch_shapes=[dma((2, 2))],
    )(both)


def fits(mesh, tokens_clean, w_query):
    n_ctx, n_tp = mesh.shape["ctx"], mesh.shape["tp"]
    heads = w_query.shape[1] // n_tp // HEAD_DIM
    tokens = tokens_clean.shape[0] // n_ctx
    return n_tp == 2 and n_ctx == 2 * heads and heads % 4 == 0 and tokens == HEAD_DIM


def solution(mesh):
    specs = dict(
        mesh=mesh,
        in_specs=(
            P(("ctx", "tp"), None),
            P(("ctx", "tp")),
            P(),
            P(),
            P(None, "tp"),
            P(None, "tp"),
            P(None, "tp"),
            P("tp", None),
            P(),
        ),
        out_specs=(P(("ctx", "tp"), None), P(("ctx", "tp"), None)),
        check_vma=False,
    )

    def layer(tokens_clean, noise_mask, mask_embed, norm_gain, w_query, w_key, w_value, w_out, block_mask):
        body = local_kernel if fits(mesh, tokens_clean, w_query) else local
        return jax.shard_map(body, **specs)(
            tokens_clean, noise_mask, mask_embed, norm_gain, w_query, w_key, w_value, w_out, block_mask)

    return layer
```

```python
import functools

import jax
import jax.numpy as jnp
import numpy as np
from jax import lax
from jax.experimental import pallas as pl
from jax.experimental.pallas import tpu as pltpu
from jax.sharding import PartitionSpec as P

HEAD_DIM = 128
BLOCK = 32


ROPE_BASE = 500000.0
EPSILON = 1e-05
NEG_FILL = -1e30


def rms_rows(values, gain):
    wide = values.astype(jnp.float32)
    factor = lax.rsqrt(jnp.mean(wide * wide, axis=-1, keepdims=True) + EPSILON)
    return (wide * factor * gain.astype(jnp.float32)).astype(jnp.bfloat16)


def rotate(values, positions):
    half_dim = values.shape[-1] // 2
    indices = jnp.arange(half_dim).astype(jnp.float32)
    freqs = ROPE_BASE ** (-2.0 * indices / values.shape[-1])
    angles = positions.astype(jnp.float32)[:, None] * freqs[None, :]
    cosine = jnp.cos(angles)[:, None, :]
    sine = jnp.sin(angles)[:, None, :]
    lower = values[..., :half_dim]
    upper = values[..., half_dim:]
    return jnp.concatenate([lower * cosine - upper * sine, upper * cosine + lower * sine], axis=-1)


def start_state(heads, length):
    return (
        jnp.full((heads, length), NEG_FILL, jnp.float32),
        jnp.zeros((heads, length), jnp.float32),
        jnp.zeros((heads, length, HEAD_DIM), jnp.float32),
    )


def attend(state, queries, keys, values, visible):
    peak_old, total_old, weighted_old = state
    scores = jnp.einsum(
        "qhd,khd->hqk", queries, keys, preferred_element_type=jnp.float32
    ) * HEAD_DIM ** (-0.5)
    scores = jnp.where(visible[None], scores, NEG_FILL)
    peak_new = jnp.maximum(peak_old, jnp.max(scores, axis=-1))
    weights = jnp.where(visible[None], jnp.exp(scores - peak_new[..., None]), 0.0)
    factor = jnp.exp(peak_old - peak_new)
    total_new = total_old * factor + jnp.sum(weights, axis=-1)
    weighted_new = weighted_old * factor[..., None] + jnp.einsum(
        "hqk,khd->hqd", weights.astype(jnp.bfloat16), values, preferred_element_type=jnp.float32
    )
    return (peak_new, total_new, weighted_new)


def local(
    tokens_clean, noise_mask, mask_embed, norm_gain, w_query, w_key, w_value, w_out, block_mask
):
    normed = rms_rows(tokens_clean, norm_gain)
    mask_row = rms_rows(mask_embed[None, :], norm_gain)
    gathered, noise_flags = (
        lax.all_gather(normed, "tp", axis=0, tiled=True),
        lax.all_gather(noise_mask, "tp", axis=0, tiled=True),
    )
    local_len = gathered.shape[0]
    width = w_query.shape[1]
    heads = width // HEAD_DIM
    first_row = lax.axis_index("ctx") * local_len
    positions = first_row + jnp.arange(local_len, dtype=jnp.int32)
    noisy_rows = (noise_flags == 1)[:, None]

    def project(weight, rotary):
        clean = jnp.dot(gathered, weight, preferred_element_type=jnp.float32)
        masked = jnp.dot(mask_row, weight, preferred_element_type=jnp.float32)
        noisy = jnp.where(noisy_rows, masked, clean)
        clean = clean.reshape(local_len, heads, HEAD_DIM)
        noisy = noisy.reshape(local_len, heads, HEAD_DIM)
        if rotary:
            clean = rotate(clean, positions)
            noisy = rotate(noisy, positions)
        return (clean.astype(jnp.bfloat16), noisy.astype(jnp.bfloat16))

    q_clean, q_noisy = project(w_query, True)
    k_clean, k_noisy = project(w_key, True)
    v_clean, v_noisy = project(w_value, False)
    key_values = jnp.stack([k_clean.reshape(local_len, width), v_clean.reshape(local_len, width)])

    def finish(state):
        weighted = state[2] / state[1][..., None]
        return jnp.transpose(weighted, (1, 0, 2)).reshape(local_len, width).astype(jnp.bfloat16)

    row_table = jnp.take(block_mask, positions // BLOCK, axis=0)
    own_block = (positions // BLOCK)[:, None] == (positions // BLOCK)[None, :]
    noisy_state = attend(start_state(heads, local_len), q_noisy, k_noisy, v_noisy, own_block)
    states = (start_state(heads, local_len), noisy_state)
    piece = lax.all_gather(key_values, "ctx", axis=1, tiled=True)
    count = piece.shape[1]
    visible = jnp.repeat(row_table, BLOCK, axis=1)
    keys = piece[0].reshape(count, heads, HEAD_DIM)
    values = piece[1].reshape(count, heads, HEAD_DIM)
    states = (
        attend(states[0], q_clean, keys, values, visible % 2 == 1),
        attend(states[1], q_noisy, keys, values, visible // 2 == 1),
    )
    attended = jnp.stack([finish(states[0]), finish(states[1])])
    model_width = w_out.shape[1]
    piece = attended
    summed = lax.psum_scatter(
        jnp.einsum("sqc,cd->qsd", piece, w_out, preferred_element_type=jnp.float32)
        .reshape(local_len // lax.axis_size("tp") * lax.axis_size("tp"), 2 * model_width)
        .astype(jnp.bfloat16),
        "tp",
        scatter_dimension=0,
        tiled=True,
    ).astype(jnp.float32)
    result = summed.reshape(summed.shape[0], 2, model_width)
    return (result[:, 0].astype(jnp.bfloat16), result[:, 1].astype(jnp.bfloat16))

LOG2E = 1.4426950408889634
MESH = pl.DeviceIdType.MESH


def layer_kernel(
    n_chips,
    x_ref, flag_ref, mask_ref, gain_ref, vis_ref, table_hbm, wq_hbm, wk_hbm, wv_hbm, wo_hbm,
    out_ref,
    w_s, wo_s, table, lhs0, lhs1, gathered, row0, row1, flags, rowall, rowin, mproj, nb, sendq, sendkv, recvq, recvkv, kall, vall, bias,
    oown, lown, obuf, lbuf, oin, lin, att, psend, precv, pown,
    wsem, wosem, tsem, xs, xr, ss, sr, cs, cr, gs, gr, ls, lc, lg, fs, fr, os_, or_, es, er, ol, el, ps, pr,
):
    ctx = lax.axis_index("ctx")
    tp = lax.axis_index("tp")
    chip = ctx // 2
    core = ctx % 2
    rows = x_ref.shape[0]
    length = 2 * rows
    pairs = n_chips // 2
    hd = HEAD_DIM
    seq = 2 * n_chips * length
    per = length // BLOCK
    my_z = chip // 2
    w_hbm = (wq_hbm, wk_hbm, wv_hbm)
    twin = {"tp": 1 - tp}
    sibling = {"ctx": 2 * chip + 1 - core}

    def pair_at(i):
        return (my_z + 2 + i) % pairs

    def w_copy(kind, i):
        cols = pl.ds(pl.multiple_of(pair_at(i) * 2 * hd, 2 * hd), 2 * hd)
        return pltpu.make_async_copy(w_hbm[kind].at[:, cols], w_s.at[kind, :, cols], wsem.at[i, kind])

    def half_rows(half):
        which = tp if half == 0 else 1 - tp
        return pl.ds(pl.multiple_of(which * rows, rows), rows)

    table_copy = pltpu.make_async_copy(table_hbm, table, tsem)
    for i in range(pairs):
        for kind in (1, 2, 0):
            w_copy(kind, i).start()
        if i == 0:
            table_copy.start()
    wo_copy = pltpu.make_async_copy(wo_hbm, wo_s, wosem)
    wo_copy.start()

    barrier = pltpu.get_barrier_semaphore()
    pl.semaphore_signal(barrier, inc=1, device_id=twin, device_id_type=MESH)
    pl.semaphore_signal(barrier, inc=1, device_id=sibling, device_id_type=MESH)
    for d in range(1, n_chips):
        peer = (chip + d) % n_chips
        pl.semaphore_signal(barrier, inc=1, device_id={"ctx": 2 * peer + core}, device_id_type=MESH)

    gain = gain_ref[...].reshape(1, x_ref.shape[1]).astype(jnp.float32)

    def norm(values):
        wide = values.astype(jnp.float32)
        factor = lax.rsqrt(jnp.mean(wide * wide, axis=-1, keepdims=True) + EPSILON)
        return (wide * factor * gain).astype(jnp.bfloat16)

    lhs0[0:rows, :] = norm(x_ref[...])
    lhs0[rows:rows + 16, :] = jnp.broadcast_to(norm(mask_ref[...].reshape(1, x_ref.shape[1])), (16, lhs0.shape[1]))
    flag_row = flag_ref[...].astype(jnp.float32).reshape(1, rows)
    row0[...] = jnp.broadcast_to(jnp.concatenate([flag_row, flag_row], axis=1), row0.shape)

    pl.semaphore_wait(barrier, n_chips + 1)

    model = x_ref.shape[1]
    cuts = (0, model // 2, 3 * model // 4, model)

    def x_copy(c):
        part = pl.ds(cuts[c], cuts[c + 1] - cuts[c])
        return pltpu.make_async_remote_copy(
            src_ref=lhs0.at[pl.ds(0, rows), part], dst_ref=lhs1.at[:, part], send_sem=xs.at[c], recv_sem=xr.at[c],
            device_id=twin, device_id_type=MESH)

    def flag_copy():
        return pltpu.make_async_remote_copy(
            src_ref=row0, dst_ref=row1, send_sem=xs.at[3], recv_sem=xr.at[3],
            device_id=twin, device_id_type=MESH)

    flag_copy().start()
    for c in range(3):
        x_copy(c).start()

    def kv_copy(head, slot, half):
        where = half_rows(half)
        return pltpu.make_async_remote_copy(
            src_ref=sendkv.at[head, where], dst_ref=recvkv.at[slot, where],
            send_sem=ss.at[head, half], recv_sem=sr.at[slot, half],
            device_id={"ctx": 2 * head + core}, device_id_type=MESH)

    def clean_copy(head, slot, half):
        where = half_rows(half)
        return pltpu.make_async_remote_copy(
            src_ref=sendq.at[0, head, where], dst_ref=recvq.at[0, slot, where],
            send_sem=cs.at[head, half], recv_sem=cr.at[slot, half],
            device_id={"ctx": 2 * head + core}, device_id_type=MESH)

    def row_copy(head, slot):
        return pltpu.make_async_remote_copy(
            src_ref=rowall, dst_ref=rowin.at[slot], send_sem=gs.at[head], recv_sem=gr.at[slot],
            device_id={"ctx": 2 * head + core}, device_id_type=MESH)

    def kv_here(half):
        where = half_rows(half)
        return pltpu.make_async_copy(sendkv.at[chip, where], recvkv.at[chip, where], ls.at[half])

    def clean_here(half):
        where = half_rows(half)
        return pltpu.make_async_copy(sendq.at[0, chip, where], recvq.at[0, chip, where], lc.at[half])

    def row_here():
        return pltpu.make_async_copy(rowall, rowin.at[chip], lg)

    def column(row):
        return jnp.transpose(jnp.broadcast_to(row, (length, length)))

    flag_copy().wait_recv()
    lane = lax.broadcasted_iota(jnp.int32, row0.shape, 1)
    rowall[...] = jnp.where(lane // rows == tp, row0[...], row1[...])
    for d in range(1, n_chips):
        row_copy((chip + d) % n_chips, chip).start()
    row_here().start()
    flags[...] = column(rowall[0:1])

    table_copy.wait()
    for half in range(2):
        if half == 1:
            key_at = lax.broadcasted_iota(jnp.int32, (vis_ref.shape[1], seq), 1)
            side = (key_at % (2 * length)) // length
            key_ctx = 2 * (key_at // (2 * length)) + jnp.where(side == 0, core, 1 - core)
            key_block = key_ctx * per + (key_at % length) // BLOCK
            spread = (lax.broadcasted_iota(jnp.int32, key_at.shape, 0) == key_block).astype(jnp.float32).astype(jnp.bfloat16)
            for copy in range(2):
                seen = ((vis_ref[...] >> copy) & 1).astype(jnp.float32).astype(jnp.bfloat16)
                shown = (jnp.dot(seen, spread, preferred_element_type=jnp.float32) - 1.0) * 1e30
                for c in range(2 * n_chips):
                    bias[c, copy] = shown[c * per:(c + 1) * per]
            for c in range(2):
                x_copy(c).wait_recv()
                part = slice(cuts[c], cuts[c + 1])

                def gather(i, carry):
                    pair = pair_at(i)
                    cols = pl.ds(pl.multiple_of(pair * 2 * hd, 2 * hd), 2 * hd)
                    for kind in range(3):
                        term = jnp.dot(lhs1[:, part], w_s[kind, part, cols], preferred_element_type=jnp.float32)
                        gathered[kind, :, cols] = term if c == 0 else gathered[kind, :, cols] + term
                    return carry

                lax.fori_loop(0, pairs, gather, 0)
            x_copy(2).wait_recv()
        where = half_rows(half)

        def project(i, carry):
            pair = pair_at(i)
            cols = pl.ds(pl.multiple_of(pair * 2 * hd, 2 * hd), 2 * hd)
            if half == 0:
                for kind in range(3):
                    w_copy(kind, i).wait()
            flag = flags[where]
            token_rows = pl.ds(pl.multiple_of(ctx * length + (tp if half == 0 else 1 - tp) * rows, rows), rows)
            cosine = table[0, token_rows]
            sine = table[1, token_rows]
            for kind in (1, 2, 0):
                if half == 0:
                    result = jnp.dot(lhs0[...], w_s[kind, :, cols], preferred_element_type=jnp.float32)
                else:
                    part = slice(cuts[2], cuts[3])
                    result = gathered[kind, :, cols] + jnp.dot(lhs1[:, part], w_s[kind, part, cols], preferred_element_type=jnp.float32)
                if half == 0:
                    mproj[kind, :, cols] = result[rows:rows + 8]
                    masked = result[rows:rows + 1]
                else:
                    masked = mproj[kind, :, cols][0:1]
                clean2 = result[0:rows]
                for k in range(2):
                    head = 2 * pair + k
                    clean = clean2[:, k * hd:(k + 1) * hd]
                    noisy = jnp.where(flag == 1.0, masked[:, k * hd:(k + 1) * hd], clean)
                    if kind < 2:
                        clean = clean * cosine + pltpu.roll(clean, hd // 2, 1) * sine
                        noisy = noisy * cosine + pltpu.roll(noisy, hd // 2, 1) * sine
                    clean = clean.astype(jnp.bfloat16)
                    noisy = noisy.astype(jnp.bfloat16)
                    if kind == 0:
                        sendq[0, head, where, :] = clean
                        sendq[1, head, where, :] = noisy
                    else:
                        nb[kind - 1, head, where, :] = noisy
                        sendkv[head, where, (kind - 1) * hd:kind * hd] = clean
                if kind != 1:
                    for k in range(2):
                        head = 2 * pair + k

                        @pl.when(head != chip)
                        def _():
                            (clean_copy if kind == 0 else kv_copy)(head, chip, half).start()

                        @pl.when(head == chip)
                        def _():
                            (clean_here if kind == 0 else kv_here)(half).start()
            return carry

        lax.fori_loop(0, pairs, project, 0)

    scale = LOG2E * hd ** -0.5
    own = (lax.broadcasted_iota(jnp.int32, (length, length), 0) // BLOCK
           == lax.broadcasted_iota(jnp.int32, (length, length), 1) // BLOCK)

    def dot_t(a, b):
        return lax.dot_general(a, b, (((1,), (1,)), ((), ())), preferred_element_type=jnp.float32)

    def share(p, kind):
        return pltpu.make_async_remote_copy(
            src_ref=recvkv.at[p, :, pl.ds(kind * hd, hd)],
            dst_ref=(kall, vall)[kind].at[p, pl.ds(length, length)],
            send_sem=fs.at[p, kind], recv_sem=fr.at[p, kind],
            device_id=sibling, device_id_type=MESH)

    def back(p, copy, slot):
        return pltpu.make_async_remote_copy(
            src_ref=obuf.at[copy, p], dst_ref=oin.at[copy, slot], send_sem=os_.at[copy, p], recv_sem=or_.at[copy, slot],
            device_id={"ctx": 2 * p + core}, device_id_type=MESH)

    def level_back(p, slot):
        return pltpu.make_async_remote_copy(
            src_ref=lbuf.at[1, p], dst_ref=lin.at[slot], send_sem=es.at[p], recv_sem=er.at[slot],
            device_id={"ctx": 2 * p + core}, device_id_type=MESH)

    def back_here(copy):
        return pltpu.make_async_copy(obuf.at[copy, chip], oin.at[copy, chip], ol.at[copy])

    def level_here():
        return pltpu.make_async_copy(lbuf.at[1, chip], lin.at[chip], el)

    for p in range(n_chips):
        for half in range(2):
            @pl.when(chip != p)
            def _():
                kv_copy(p, p, half).wait_recv()

            @pl.when(chip == p)
            def _():
                kv_here(half).wait()
        for kind in range(2):
            share(p, kind).start()
        kall[p, 0:length, :] = recvkv[p, :, 0:hd]
        vall[p, 0:length, :] = recvkv[p, :, hd:2 * hd]
    for p in range(n_chips):
        for kind in range(2):
            share(p, kind).wait_recv()

    chunks = psend.shape[1]
    width = psend.shape[3]

    def term_copy(copy, j):
        return pltpu.make_async_remote_copy(
            src_ref=psend.at[copy, j], dst_ref=precv.at[copy, j], send_sem=ps.at[copy, j], recv_sem=pr.at[copy, j],
            device_id=twin, device_id_type=MESH)

    def out_cols(j):
        return pl.ds(pl.multiple_of(j * width, width), width)

    def project_out(copy):
        mine = half_rows(0)
        theirs = half_rows(1)
        for head in range(n_chips):
            @pl.when(chip != head)
            def _():
                back(head, copy, head).wait_recv()

            @pl.when(chip == head)
            def _():
                back_here(copy).wait()
            if copy == 1:
                @pl.when(chip != head)
                def _():
                    level_back(head, head).wait_recv()

                @pl.when(chip == head)
                def _():
                    level_here().wait()
                away = jnp.transpose(jnp.broadcast_to(lin[head][0:1], (length, hd)))
                home = lown[head]
                top = jnp.maximum(away, home)
                w_away = jnp.exp2(away - top)
                w_home = jnp.exp2(home - top)
                noisy = oin[1, head].astype(jnp.float32)
                noisy = (noisy * w_away + oown[head] * w_home) / (w_away + w_home)
                oin[1, head] = noisy.astype(jnp.bfloat16)
            cols = slice(head * hd, (head + 1) * hd)
            att[copy, 0:rows, cols] = oin[copy, head, theirs, :]
            att[copy, rows:length, cols] = oin[copy, head, mine, :]

        def term(j, carry):
            both = jnp.dot(att[copy], wo_s[:, out_cols(j)], preferred_element_type=jnp.float32).astype(jnp.bfloat16)
            psend[copy, j] = both[0:rows]
            pown[copy, j] = both[rows:length]
            term_copy(copy, j).start()
            return carry

        lax.fori_loop(0, chunks, term, 0)

    def attend_step(step, carry):
        copy = step // pairs
        low = (my_z + step) % pairs
        chosen = (low, n_chips - 1 - low)
        for p in chosen:
            @pl.when((copy == 0) & (chip != p))
            def _():
                for half in range(2):
                    clean_copy(p, p, half).wait_recv()
                row_copy(p, p).wait_recv()

            @pl.when((copy == 0) & (chip == p))
            def _():
                for half in range(2):
                    clean_here(half).wait()
                row_here().wait()

            @pl.when(copy == 1)
            def _():
                token_rows = pl.ds(pl.multiple_of((2 * p + core) * length, length), length)
                masked = jnp.broadcast_to(mproj[0, :, pl.ds(pl.multiple_of(chip * hd, hd), hd)][0:1], (length, hd))
                masked = masked * table[0, token_rows] + pltpu.roll(masked, hd // 2, 1) * table[1, token_rows]
                clean = recvq[0, p].astype(jnp.float32)
                recvq[1, p] = jnp.where(column(rowin[p][0:1]) == 1.0, masked, clean).astype(jnp.bfloat16)

        for k in range(pairs):
            @pl.when(low == k)
            def _():
                for q in (k, n_chips - 1 - k):
                    count = (q + 1) * 2 * length
                    keys = kall[0:q + 1].reshape(count, hd)
                    values = vall[0:q + 1].reshape(count, hd)
                    shown = bias[2 * q + core, copy][:, 0:count]
                    extra = jnp.concatenate(
                        [jnp.broadcast_to(shown[b:b + 1], (BLOCK, count)) for b in range(per)], axis=0)
                    scores = dot_t(recvq[copy, q], keys) * scale + extra
                    peak = jnp.max(scores, axis=-1, keepdims=True)
                    weights = jnp.exp2(scores - peak)
                    total = jnp.sum(weights, axis=-1, keepdims=True)
                    result = jnp.dot(weights.astype(jnp.bfloat16), values, preferred_element_type=jnp.float32) / total
                    obuf[copy, q] = result.astype(jnp.bfloat16)
                    level = jnp.broadcast_to(peak + jnp.log(total) * LOG2E, (length, hd))
                    lbuf[copy, q] = jnp.transpose(level)[0:8]

        for p in chosen:
            @pl.when(chip != p)
            def _():
                back(p, copy, chip).start()

            @pl.when(chip == p)
            def _():
                back_here(copy).start()

            @pl.when((copy == 1) & (chip != p))
            def _():
                level_back(p, chip).start()

            @pl.when((copy == 1) & (chip == p))
            def _():
                level_here().start()

        @pl.when(step == pairs + pairs // 2 - 1)
        def _():
            wo_copy.wait()
            project_out(0)
        return carry

    lax.fori_loop(0, 2 * pairs, attend_step, 0)
    for head in range(n_chips):
        scores = jnp.where(own, dot_t(sendq[1, head], nb[0, head]) * scale, NEG_FILL)
        peak = jnp.max(scores, axis=-1, keepdims=True)
        weights = jnp.exp2(scores - peak)
        total = jnp.sum(weights, axis=-1, keepdims=True)
        oown[head] = jnp.dot(weights.astype(jnp.bfloat16), nb[1, head], preferred_element_type=jnp.float32) / total
        lown[head] = jnp.broadcast_to(peak + jnp.log(total) * LOG2E, (length, hd))
    project_out(1)

    for copy in range(2):
        def total_of(j, carry):
            term_copy(copy, j).wait_recv()
            summed = pown[copy, j].astype(jnp.float32) + precv[copy, j].astype(jnp.float32)
            out_ref[copy, :, out_cols(j)] = summed.astype(jnp.bfloat16)
            return carry

        lax.fori_loop(0, chunks, total_of, 0)

    flag_copy().wait_send()
    for c in range(3):
        x_copy(c).wait_send()
    for p in range(n_chips):
        for kind in range(2):
            share(p, kind).wait_send()

        @pl.when(chip != p)
        def _():
            for half in range(2):
                kv_copy(p, chip, half).wait_send()
                clean_copy(p, chip, half).wait_send()
            row_copy(p, chip).wait_send()
            for copy in range(2):
                back(p, copy, chip).wait_send()
            level_back(p, chip).wait_send()
    for copy in range(2):
        for j in range(chunks):
            term_copy(copy, j).wait_send()


def place_kernel(both, clean, noisy):
    clean[...] = both[0]
    noisy[...] = both[1]


def rotary_table(length):
    indices = np.arange(HEAD_DIM // 2).astype(np.float32)
    freqs = (ROPE_BASE ** (-2.0 * indices.astype(np.float64) / HEAD_DIM)).astype(np.float32)
    angles = (np.arange(length, dtype=np.float32)[:, None] * freqs[None, :]).astype(np.float64)
    cosine = np.cos(angles).astype(np.float32)
    sine = np.sin(angles).astype(np.float32)
    return np.stack([np.concatenate([cosine, cosine], axis=1), np.concatenate([-sine, sine], axis=1)])


def local_kernel(
    tokens_clean, noise_mask, mask_embed, norm_gain, w_query, w_key, w_value, w_out, block_mask
):
    rows, model = tokens_clean.shape
    length = 2 * rows
    width = w_query.shape[1]
    n_chips = width // HEAD_DIM
    hd = HEAD_DIM
    seq = 2 * n_chips * length
    per = length // BLOCK
    bf, f32 = jnp.bfloat16, jnp.float32
    chunks = 8
    part = model // chunks
    dma = pltpu.SemaphoreType.DMA
    vmem = pl.BlockSpec(memory_space=pltpu.VMEM)
    hbm = pl.BlockSpec(memory_space=pl.ANY)
    both = pl.pallas_call(
        functools.partial(layer_kernel, n_chips),
        out_shape=jax.ShapeDtypeStruct((2, rows, model), bf),
        in_specs=[vmem] * 5 + [hbm] * 5,
        out_specs=vmem,
        scratch_shapes=[
            pltpu.VMEM((3, model, width), bf),
            pltpu.VMEM((width, model), bf),
            pltpu.VMEM((2, seq, hd), f32),
            pltpu.VMEM((rows + 16, model), bf),
            pltpu.VMEM((rows, model), bf),
            pltpu.VMEM((3, rows, width), f32),
            pltpu.VMEM((8, length), f32),
            pltpu.VMEM((8, length), f32),
            pltpu.VMEM((length, hd), f32),
            pltpu.VMEM((8, length), f32),
            pltpu.VMEM((n_chips, 8, length), f32),
            pltpu.VMEM((3, 8, width), f32),
            pltpu.VMEM((2, n_chips, length, hd), bf),
            pltpu.VMEM((2, n_chips, length, hd), bf),
            pltpu.VMEM((n_chips, length, 2 * hd), bf),
            pltpu.VMEM((2, n_chips, length, hd), bf),
            pltpu.VMEM((n_chips, length, 2 * hd), bf),
            pltpu.VMEM((n_chips, 2 * length, hd), bf),
            pltpu.VMEM((n_chips, 2 * length, hd), bf),
            pltpu.VMEM((2 * n_chips, 2, per, seq), f32),
            pltpu.VMEM((n_chips, length, hd), f32),
            pltpu.VMEM((n_chips, length, hd), f32),
            pltpu.VMEM((2, n_chips, length, hd), bf),
            pltpu.VMEM((2, n_chips, 8, hd), f32),
            pltpu.VMEM((2, n_chips, length, hd), bf),
            pltpu.VMEM((n_chips, 8, hd), f32),
            pltpu.VMEM((2, length, width), bf),
            pltpu.VMEM((2, chunks, rows, part), bf),
            pltpu.VMEM((2, chunks, rows, part), bf),
            pltpu.VMEM((2, chunks, rows, part), bf),
            dma((n_chips // 2, 3)),
            dma,
            dma,
            dma((4,)),
            dma((4,)),
            dma((n_chips, 2)),
            dma((n_chips, 2)),
            dma((n_chips, 2)),
            dma((n_chips, 2)),
            dma((n_chips,)),
            dma((n_chips,)),
            dma((2,)),
            dma((2,)),
            dma,
            dma((n_chips, 2)),
            dma((n_chips, 2)),
            dma((2, n_chips)),
            dma((2, n_chips)),
            dma((n_chips,)),
            dma((n_chips,)),
            dma((2,)),
            dma,
            dma((2, chunks)),
            dma((2, chunks)),
        ],
        compiler_params=pltpu.CompilerParams(
            collective_id=0, has_side_effects=True, vmem_limit_bytes=60 * 1024 * 1024),
        cost_estimate=pl.CostEstimate(flops=6 * 10**9, bytes_accessed=34 * 2**20, transcendentals=3 * 10**6),
    )(tokens_clean, noise_mask, mask_embed, norm_gain, block_mask, jnp.asarray(rotary_table(seq)),
      w_query, w_key, w_value, w_out)
    return pl.pallas_call(
        place_kernel,
        out_shape=(jax.ShapeDtypeStruct((rows, model), bf), jax.ShapeDtypeStruct((rows, model), bf)),
        in_specs=[vmem],
        out_specs=(vmem, vmem),
    )(both)


def fits(mesh, tokens_clean, w_query):
    n_ctx, n_tp = mesh.shape["ctx"], mesh.shape["tp"]
    heads = w_query.shape[1] // n_tp // HEAD_DIM
    tokens = tokens_clean.shape[0] // n_ctx
    return n_tp == 2 and n_ctx == 2 * heads and heads % 4 == 0 and tokens == HEAD_DIM


def solution(mesh):
    specs = dict(
        mesh=mesh,
        in_specs=(
            P(("ctx", "tp"), None),
            P(("ctx", "tp")),
            P(),
            P(),
            P(None, "tp"),
            P(None, "tp"),
            P(None, "tp"),
            P("tp", None),
            P(),
        ),
        out_specs=(P(("ctx", "tp"), None), P(("ctx", "tp"), None)),
        check_vma=False,
    )

    def layer(tokens_clean, noise_mask, mask_embed, norm_gain, w_query, w_key, w_value, w_out, block_mask):
        body = local_kernel if fits(mesh, tokens_clean, w_query) else local
        return jax.shard_map(body, **specs)(
            tokens_clean, noise_mask, mask_embed, norm_gain, w_query, w_key, w_value, w_out, block_mask)

    return layer
```

```python
import functools

import jax
import jax.numpy as jnp
import numpy as np
from jax import lax
from jax.experimental import pallas as pl
from jax.experimental.pallas import tpu as pltpu
from jax.sharding import PartitionSpec as P

HEAD_DIM = 128
BLOCK = 32


ROPE_BASE = 500000.0
EPSILON = 1e-05
NEG_FILL = -1e30


def rms_rows(values, gain):
    wide = values.astype(jnp.float32)
    factor = lax.rsqrt(jnp.mean(wide * wide, axis=-1, keepdims=True) + EPSILON)
    return (wide * factor * gain.astype(jnp.float32)).astype(jnp.bfloat16)


def rotate(values, positions):
    half_dim = values.shape[-1] // 2
    indices = jnp.arange(half_dim).astype(jnp.float32)
    freqs = ROPE_BASE ** (-2.0 * indices / values.shape[-1])
    angles = positions.astype(jnp.float32)[:, None] * freqs[None, :]
    cosine = jnp.cos(angles)[:, None, :]
    sine = jnp.sin(angles)[:, None, :]
    lower = values[..., :half_dim]
    upper = values[..., half_dim:]
    return jnp.concatenate([lower * cosine - upper * sine, upper * cosine + lower * sine], axis=-1)


def start_state(heads, length):
    return (
        jnp.full((heads, length), NEG_FILL, jnp.float32),
        jnp.zeros((heads, length), jnp.float32),
        jnp.zeros((heads, length, HEAD_DIM), jnp.float32),
    )


def attend(state, queries, keys, values, visible):
    peak_old, total_old, weighted_old = state
    scores = jnp.einsum(
        "qhd,khd->hqk", queries, keys, preferred_element_type=jnp.float32
    ) * HEAD_DIM ** (-0.5)
    scores = jnp.where(visible[None], scores, NEG_FILL)
    peak_new = jnp.maximum(peak_old, jnp.max(scores, axis=-1))
    weights = jnp.where(visible[None], jnp.exp(scores - peak_new[..., None]), 0.0)
    factor = jnp.exp(peak_old - peak_new)
    total_new = total_old * factor + jnp.sum(weights, axis=-1)
    weighted_new = weighted_old * factor[..., None] + jnp.einsum(
        "hqk,khd->hqd", weights.astype(jnp.bfloat16), values, preferred_element_type=jnp.float32
    )
    return (peak_new, total_new, weighted_new)


def local(
    tokens_clean, noise_mask, mask_embed, norm_gain, w_query, w_key, w_value, w_out, block_mask
):
    normed = rms_rows(tokens_clean, norm_gain)
    mask_row = rms_rows(mask_embed[None, :], norm_gain)
    gathered, noise_flags = (
        lax.all_gather(normed, "tp", axis=0, tiled=True),
        lax.all_gather(noise_mask, "tp", axis=0, tiled=True),
    )
    local_len = gathered.shape[0]
    width = w_query.shape[1]
    heads = width // HEAD_DIM
    first_row = lax.axis_index("ctx") * local_len
    positions = first_row + jnp.arange(local_len, dtype=jnp.int32)
    noisy_rows = (noise_flags == 1)[:, None]

    def project(weight, rotary):
        clean = jnp.dot(gathered, weight, preferred_element_type=jnp.float32)
        masked = jnp.dot(mask_row, weight, preferred_element_type=jnp.float32)
        noisy = jnp.where(noisy_rows, masked, clean)
        clean = clean.reshape(local_len, heads, HEAD_DIM)
        noisy = noisy.reshape(local_len, heads, HEAD_DIM)
        if rotary:
            clean = rotate(clean, positions)
            noisy = rotate(noisy, positions)
        return (clean.astype(jnp.bfloat16), noisy.astype(jnp.bfloat16))

    q_clean, q_noisy = project(w_query, True)
    k_clean, k_noisy = project(w_key, True)
    v_clean, v_noisy = project(w_value, False)
    key_values = jnp.stack([k_clean.reshape(local_len, width), v_clean.reshape(local_len, width)])

    def finish(state):
        weighted = state[2] / state[1][..., None]
        return jnp.transpose(weighted, (1, 0, 2)).reshape(local_len, width).astype(jnp.bfloat16)

    row_table = jnp.take(block_mask, positions // BLOCK, axis=0)
    own_block = (positions // BLOCK)[:, None] == (positions // BLOCK)[None, :]
    noisy_state = attend(start_state(heads, local_len), q_noisy, k_noisy, v_noisy, own_block)
    states = (start_state(heads, local_len), noisy_state)
    piece = lax.all_gather(key_values, "ctx", axis=1, tiled=True)
    count = piece.shape[1]
    visible = jnp.repeat(row_table, BLOCK, axis=1)
    keys = piece[0].reshape(count, heads, HEAD_DIM)
    values = piece[1].reshape(count, heads, HEAD_DIM)
    states = (
        attend(states[0], q_clean, keys, values, visible % 2 == 1),
        attend(states[1], q_noisy, keys, values, visible // 2 == 1),
    )
    attended = jnp.stack([finish(states[0]), finish(states[1])])
    model_width = w_out.shape[1]
    piece = attended
    summed = lax.psum_scatter(
        jnp.einsum("sqc,cd->qsd", piece, w_out, preferred_element_type=jnp.float32)
        .reshape(local_len // lax.axis_size("tp") * lax.axis_size("tp"), 2 * model_width)
        .astype(jnp.bfloat16),
        "tp",
        scatter_dimension=0,
        tiled=True,
    ).astype(jnp.float32)
    result = summed.reshape(summed.shape[0], 2, model_width)
    return (result[:, 0].astype(jnp.bfloat16), result[:, 1].astype(jnp.bfloat16))

LOG2E = 1.4426950408889634
MESH = pl.DeviceIdType.MESH


def layer_kernel(
    n_chips,
    x_ref, flag_ref, mask_ref, gain_ref, vis_ref, table_hbm, wq_hbm, wk_hbm, wv_hbm, wo_hbm,
    out_ref,
    w_s, wo_s, table, lhs0, lhs1, row0, row1, flags, rowall, rowin, mproj, nb, sendq, sendkv, recvq, recvkv, kall, vall, bias,
    oown, lown, obuf, lbuf, oin, lin, att, psend, precv, pown,
    wsem, wosem, tsem, xs, xr, ss, sr, cs, cr, gs, gr, ls, lc, lg, fs, fr, os_, or_, es, er, ol, el, ps, pr,
):
    ctx = lax.axis_index("ctx")
    tp = lax.axis_index("tp")
    chip = ctx // 2
    core = ctx % 2
    rows = x_ref.shape[0]
    length = 2 * rows
    pairs = n_chips // 2
    hd = HEAD_DIM
    seq = 2 * n_chips * length
    per = length // BLOCK
    my_z = chip // 2
    w_hbm = (wq_hbm, wk_hbm, wv_hbm)
    twin = {"tp": 1 - tp}
    sibling = {"ctx": 2 * chip + 1 - core}

    def pair_at(i):
        return (my_z + 2 + i) % pairs

    def w_copy(kind, i):
        cols = pl.ds(pl.multiple_of(pair_at(i) * 2 * hd, 2 * hd), 2 * hd)
        return pltpu.make_async_copy(w_hbm[kind].at[:, cols], w_s.at[kind, :, cols], wsem.at[i, kind])

    def half_rows(half):
        which = tp if half == 0 else 1 - tp
        return pl.ds(pl.multiple_of(which * rows, rows), rows)

    table_copy = pltpu.make_async_copy(table_hbm, table, tsem)
    for i in range(pairs):
        for kind in (1, 2, 0):
            w_copy(kind, i).start()
        if i == 0:
            table_copy.start()
    wo_copy = pltpu.make_async_copy(wo_hbm, wo_s, wosem)
    wo_copy.start()

    barrier = pltpu.get_barrier_semaphore()
    pl.semaphore_signal(barrier, inc=1, device_id=twin, device_id_type=MESH)
    pl.semaphore_signal(barrier, inc=1, device_id=sibling, device_id_type=MESH)
    for d in range(1, n_chips):
        peer = (chip + d) % n_chips
        pl.semaphore_signal(barrier, inc=1, device_id={"ctx": 2 * peer + core}, device_id_type=MESH)

    gain = gain_ref[...].reshape(1, x_ref.shape[1]).astype(jnp.float32)

    def norm(values):
        wide = values.astype(jnp.float32)
        factor = lax.rsqrt(jnp.mean(wide * wide, axis=-1, keepdims=True) + EPSILON)
        return (wide * factor * gain).astype(jnp.bfloat16)

    lhs0[0:rows, :] = norm(x_ref[...])
    lhs0[rows:rows + 16, :] = jnp.broadcast_to(norm(mask_ref[...].reshape(1, x_ref.shape[1])), (16, lhs0.shape[1]))
    flag_row = flag_ref[...].astype(jnp.float32).reshape(1, rows)
    row0[...] = jnp.broadcast_to(jnp.concatenate([flag_row, flag_row], axis=1), row0.shape)

    pl.semaphore_wait(barrier, n_chips + 1)

    def x_copy():
        return pltpu.make_async_remote_copy(
            src_ref=lhs0.at[pl.ds(0, rows)], dst_ref=lhs1, send_sem=xs.at[0], recv_sem=xr.at[0],
            device_id=twin, device_id_type=MESH)

    def flag_copy():
        return pltpu.make_async_remote_copy(
            src_ref=row0, dst_ref=row1, send_sem=xs.at[1], recv_sem=xr.at[1],
            device_id=twin, device_id_type=MESH)

    flag_copy().start()
    x_copy().start()

    def kv_copy(head, slot, half):
        where = half_rows(half)
        return pltpu.make_async_remote_copy(
            src_ref=sendkv.at[head, where], dst_ref=recvkv.at[slot, where],
            send_sem=ss.at[head, half], recv_sem=sr.at[slot, half],
            device_id={"ctx": 2 * head + core}, device_id_type=MESH)

    def clean_copy(head, slot, half):
        where = half_rows(half)
        return pltpu.make_async_remote_copy(
            src_ref=sendq.at[0, head, where], dst_ref=recvq.at[0, slot, where],
            send_sem=cs.at[head, half], recv_sem=cr.at[slot, half],
            device_id={"ctx": 2 * head + core}, device_id_type=MESH)

    def row_copy(head, slot):
        return pltpu.make_async_remote_copy(
            src_ref=rowall, dst_ref=rowin.at[slot], send_sem=gs.at[head], recv_sem=gr.at[slot],
            device_id={"ctx": 2 * head + core}, device_id_type=MESH)

    def kv_here(half):
        where = half_rows(half)
        return pltpu.make_async_copy(sendkv.at[chip, where], recvkv.at[chip, where], ls.at[half])

    def clean_here(half):
        where = half_rows(half)
        return pltpu.make_async_copy(sendq.at[0, chip, where], recvq.at[0, chip, where], lc.at[half])

    def row_here():
        return pltpu.make_async_copy(rowall, rowin.at[chip], lg)

    def column(row):
        return jnp.transpose(jnp.broadcast_to(row, (length, length)))

    flag_copy().wait_recv()
    lane = lax.broadcasted_iota(jnp.int32, row0.shape, 1)
    rowall[...] = jnp.where(lane // rows == tp, row0[...], row1[...])
    for d in range(1, n_chips):
        row_copy((chip + d) % n_chips, chip).start()
    row_here().start()
    flags[...] = column(rowall[0:1])

    table_copy.wait()
    for half in range(2):
        if half == 1:
            x_copy().wait_recv()
        where = half_rows(half)

        def project(i, carry):
            pair = pair_at(i)
            cols = pl.ds(pl.multiple_of(pair * 2 * hd, 2 * hd), 2 * hd)
            if half == 0:
                for kind in range(3):
                    w_copy(kind, i).wait()
            flag = flags[where]
            token_rows = pl.ds(pl.multiple_of(ctx * length + (tp if half == 0 else 1 - tp) * rows, rows), rows)
            cosine = table[0, token_rows]
            sine = table[1, token_rows]
            for kind in (1, 2, 0):
                left = (lhs0 if half == 0 else lhs1)[...]
                result = jnp.dot(left, w_s[kind, :, cols], preferred_element_type=jnp.float32)
                if half == 0:
                    mproj[kind, :, cols] = result[rows:rows + 8]
                    masked = result[rows:rows + 1]
                else:
                    masked = mproj[kind, :, cols][0:1]
                clean2 = result[0:rows]
                for k in range(2):
                    head = 2 * pair + k
                    clean = clean2[:, k * hd:(k + 1) * hd]
                    noisy = jnp.where(flag == 1.0, masked[:, k * hd:(k + 1) * hd], clean)
                    if kind < 2:
                        clean = clean * cosine + pltpu.roll(clean, hd // 2, 1) * sine
                        noisy = noisy * cosine + pltpu.roll(noisy, hd // 2, 1) * sine
                    clean = clean.astype(jnp.bfloat16)
                    noisy = noisy.astype(jnp.bfloat16)
                    if kind == 0:
                        sendq[0, head, where, :] = clean
                        sendq[1, head, where, :] = noisy
                    else:
                        nb[kind - 1, head, where, :] = noisy
                        sendkv[head, where, (kind - 1) * hd:kind * hd] = clean
                if kind != 1:
                    for k in range(2):
                        head = 2 * pair + k

                        @pl.when(head != chip)
                        def _():
                            (clean_copy if kind == 0 else kv_copy)(head, chip, half).start()

                        @pl.when(head == chip)
                        def _():
                            (clean_here if kind == 0 else kv_here)(half).start()
            return carry

        lax.fori_loop(0, pairs, project, 0)

    key_at = lax.broadcasted_iota(jnp.int32, (vis_ref.shape[1], seq), 1)
    side = (key_at % (2 * length)) // length
    key_ctx = 2 * (key_at // (2 * length)) + jnp.where(side == 0, core, 1 - core)
    key_block = key_ctx * per + (key_at % length) // BLOCK
    spread = (lax.broadcasted_iota(jnp.int32, key_at.shape, 0) == key_block).astype(jnp.float32).astype(jnp.bfloat16)
    for copy in range(2):
        seen = ((vis_ref[...] >> copy) & 1).astype(jnp.float32).astype(jnp.bfloat16)
        shown = (jnp.dot(seen, spread, preferred_element_type=jnp.float32) - 1.0) * 1e30
        for c in range(2 * n_chips):
            bias[c, copy] = shown[c * per:(c + 1) * per]

    scale = LOG2E * hd ** -0.5
    own = (lax.broadcasted_iota(jnp.int32, (length, length), 0) // BLOCK
           == lax.broadcasted_iota(jnp.int32, (length, length), 1) // BLOCK)

    def dot_t(a, b):
        return lax.dot_general(a, b, (((1,), (1,)), ((), ())), preferred_element_type=jnp.float32)

    for head in range(n_chips):
        scores = jnp.where(own, dot_t(sendq[1, head], nb[0, head]) * scale, NEG_FILL)
        peak = jnp.max(scores, axis=-1, keepdims=True)
        weights = jnp.exp2(scores - peak)
        total = jnp.sum(weights, axis=-1, keepdims=True)
        oown[head] = jnp.dot(weights.astype(jnp.bfloat16), nb[1, head], preferred_element_type=jnp.float32) / total
        lown[head] = jnp.broadcast_to(peak + jnp.log(total) * LOG2E, (length, hd))

    def share(p, kind):
        return pltpu.make_async_remote_copy(
            src_ref=recvkv.at[p, :, pl.ds(kind * hd, hd)],
            dst_ref=(kall, vall)[kind].at[p, pl.ds(length, length)],
            send_sem=fs.at[p, kind], recv_sem=fr.at[p, kind],
            device_id=sibling, device_id_type=MESH)

    def back(p, copy, slot):
        return pltpu.make_async_remote_copy(
            src_ref=obuf.at[copy, p], dst_ref=oin.at[copy, slot], send_sem=os_.at[copy, p], recv_sem=or_.at[copy, slot],
            device_id={"ctx": 2 * p + core}, device_id_type=MESH)

    def level_back(p, slot):
        return pltpu.make_async_remote_copy(
            src_ref=lbuf.at[1, p], dst_ref=lin.at[slot], send_sem=es.at[p], recv_sem=er.at[slot],
            device_id={"ctx": 2 * p + core}, device_id_type=MESH)

    def back_here(copy):
        return pltpu.make_async_copy(obuf.at[copy, chip], oin.at[copy, chip], ol.at[copy])

    def level_here():
        return pltpu.make_async_copy(lbuf.at[1, chip], lin.at[chip], el)

    for p in range(n_chips):
        for half in range(2):
            @pl.when(chip != p)
            def _():
                kv_copy(p, p, half).wait_recv()

            @pl.when(chip == p)
            def _():
                kv_here(half).wait()
        for kind in range(2):
            share(p, kind).start()
        kall[p, 0:length, :] = recvkv[p, :, 0:hd]
        vall[p, 0:length, :] = recvkv[p, :, hd:2 * hd]
    for p in range(n_chips):
        for kind in range(2):
            share(p, kind).wait_recv()

    chunks = psend.shape[1]
    width = psend.shape[3]

    def term_copy(copy, j):
        return pltpu.make_async_remote_copy(
            src_ref=psend.at[copy, j], dst_ref=precv.at[copy, j], send_sem=ps.at[copy, j], recv_sem=pr.at[copy, j],
            device_id=twin, device_id_type=MESH)

    def out_cols(j):
        return pl.ds(pl.multiple_of(j * width, width), width)

    def project_out(copy):
        mine = half_rows(0)
        theirs = half_rows(1)
        for head in range(n_chips):
            @pl.when(chip != head)
            def _():
                back(head, copy, head).wait_recv()

            @pl.when(chip == head)
            def _():
                back_here(copy).wait()
            if copy == 1:
                @pl.when(chip != head)
                def _():
                    level_back(head, head).wait_recv()

                @pl.when(chip == head)
                def _():
                    level_here().wait()
                away = jnp.transpose(jnp.broadcast_to(lin[head][0:1], (length, hd)))
                home = lown[head]
                top = jnp.maximum(away, home)
                w_away = jnp.exp2(away - top)
                w_home = jnp.exp2(home - top)
                noisy = oin[1, head].astype(jnp.float32)
                noisy = (noisy * w_away + oown[head] * w_home) / (w_away + w_home)
                oin[1, head] = noisy.astype(jnp.bfloat16)
            cols = slice(head * hd, (head + 1) * hd)
            att[copy, 0:rows, cols] = oin[copy, head, theirs, :]
            att[copy, rows:length, cols] = oin[copy, head, mine, :]

        def term(j, carry):
            both = jnp.dot(att[copy], wo_s[:, out_cols(j)], preferred_element_type=jnp.float32).astype(jnp.bfloat16)
            psend[copy, j] = both[0:rows]
            pown[copy, j] = both[rows:length]
            term_copy(copy, j).start()
            return carry

        lax.fori_loop(0, chunks, term, 0)

    def attend_step(step, carry):
        copy = step // pairs
        low = (my_z + step) % pairs
        chosen = (low, n_chips - 1 - low)
        for p in chosen:
            @pl.when((copy == 0) & (chip != p))
            def _():
                for half in range(2):
                    clean_copy(p, p, half).wait_recv()
                row_copy(p, p).wait_recv()

            @pl.when((copy == 0) & (chip == p))
            def _():
                for half in range(2):
                    clean_here(half).wait()
                row_here().wait()

            @pl.when(copy == 1)
            def _():
                token_rows = pl.ds(pl.multiple_of((2 * p + core) * length, length), length)
                masked = jnp.broadcast_to(mproj[0, :, pl.ds(pl.multiple_of(chip * hd, hd), hd)][0:1], (length, hd))
                masked = masked * table[0, token_rows] + pltpu.roll(masked, hd // 2, 1) * table[1, token_rows]
                clean = recvq[0, p].astype(jnp.float32)
                recvq[1, p] = jnp.where(column(rowin[p][0:1]) == 1.0, masked, clean).astype(jnp.bfloat16)

        for k in range(pairs):
            @pl.when(low == k)
            def _():
                for q in (k, n_chips - 1 - k):
                    count = (q + 1) * 2 * length
                    keys = kall[0:q + 1].reshape(count, hd)
                    values = vall[0:q + 1].reshape(count, hd)
                    shown = bias[2 * q + core, copy][:, 0:count]
                    extra = jnp.concatenate(
                        [jnp.broadcast_to(shown[b:b + 1], (BLOCK, count)) for b in range(per)], axis=0)
                    scores = dot_t(recvq[copy, q], keys) * scale + extra
                    peak = jnp.max(scores, axis=-1, keepdims=True)
                    weights = jnp.exp2(scores - peak)
                    total = jnp.sum(weights, axis=-1, keepdims=True)
                    result = jnp.dot(weights.astype(jnp.bfloat16), values, preferred_element_type=jnp.float32) / total
                    obuf[copy, q] = result.astype(jnp.bfloat16)
                    level = jnp.broadcast_to(peak + jnp.log(total) * LOG2E, (length, hd))
                    lbuf[copy, q] = jnp.transpose(level)[0:8]

        for p in chosen:
            @pl.when(chip != p)
            def _():
                back(p, copy, chip).start()

            @pl.when(chip == p)
            def _():
                back_here(copy).start()

            @pl.when((copy == 1) & (chip != p))
            def _():
                level_back(p, chip).start()

            @pl.when((copy == 1) & (chip == p))
            def _():
                level_here().start()

        @pl.when(step == pairs + pairs // 2 - 1)
        def _():
            wo_copy.wait()
            project_out(0)
        return carry

    lax.fori_loop(0, 2 * pairs, attend_step, 0)
    project_out(1)

    for copy in range(2):
        def total_of(j, carry):
            term_copy(copy, j).wait_recv()
            summed = pown[copy, j].astype(jnp.float32) + precv[copy, j].astype(jnp.float32)
            out_ref[copy, :, out_cols(j)] = summed.astype(jnp.bfloat16)
            return carry

        lax.fori_loop(0, chunks, total_of, 0)

    flag_copy().wait_send()
    x_copy().wait_send()
    for p in range(n_chips):
        for kind in range(2):
            share(p, kind).wait_send()

        @pl.when(chip != p)
        def _():
            for half in range(2):
                kv_copy(p, chip, half).wait_send()
                clean_copy(p, chip, half).wait_send()
            row_copy(p, chip).wait_send()
            for copy in range(2):
                back(p, copy, chip).wait_send()
            level_back(p, chip).wait_send()
    for copy in range(2):
        for j in range(chunks):
            term_copy(copy, j).wait_send()


def place_kernel(both, clean, noisy):
    clean[...] = both[0]
    noisy[...] = both[1]


def rotary_table(length):
    indices = np.arange(HEAD_DIM // 2).astype(np.float32)
    freqs = (ROPE_BASE ** (-2.0 * indices.astype(np.float64) / HEAD_DIM)).astype(np.float32)
    angles = (np.arange(length, dtype=np.float32)[:, None] * freqs[None, :]).astype(np.float64)
    cosine = np.cos(angles).astype(np.float32)
    sine = np.sin(angles).astype(np.float32)
    return np.stack([np.concatenate([cosine, cosine], axis=1), np.concatenate([-sine, sine], axis=1)])


def local_kernel(
    tokens_clean, noise_mask, mask_embed, norm_gain, w_query, w_key, w_value, w_out, block_mask
):
    rows, model = tokens_clean.shape
    length = 2 * rows
    width = w_query.shape[1]
    n_chips = width // HEAD_DIM
    hd = HEAD_DIM
    seq = 2 * n_chips * length
    per = length // BLOCK
    bf, f32 = jnp.bfloat16, jnp.float32
    chunks = 8
    part = model // chunks
    dma = pltpu.SemaphoreType.DMA
    vmem = pl.BlockSpec(memory_space=pltpu.VMEM)
    hbm = pl.BlockSpec(memory_space=pl.ANY)
    both = pl.pallas_call(
        functools.partial(layer_kernel, n_chips),
        out_shape=jax.ShapeDtypeStruct((2, rows, model), bf),
        in_specs=[vmem] * 5 + [hbm] * 5,
        out_specs=vmem,
        scratch_shapes=[
            pltpu.VMEM((3, model, width), bf),
            pltpu.VMEM((width, model), bf),
            pltpu.VMEM((2, seq, hd), f32),
            pltpu.VMEM((rows + 16, model), bf),
            pltpu.VMEM((rows, model), bf),
            pltpu.VMEM((8, length), f32),
            pltpu.VMEM((8, length), f32),
            pltpu.VMEM((length, hd), f32),
            pltpu.VMEM((8, length), f32),
            pltpu.VMEM((n_chips, 8, length), f32),
            pltpu.VMEM((3, 8, width), f32),
            pltpu.VMEM((2, n_chips, length, hd), bf),
            pltpu.VMEM((2, n_chips, length, hd), bf),
            pltpu.VMEM((n_chips, length, 2 * hd), bf),
            pltpu.VMEM((2, n_chips, length, hd), bf),
            pltpu.VMEM((n_chips, length, 2 * hd), bf),
            pltpu.VMEM((n_chips, 2 * length, hd), bf),
            pltpu.VMEM((n_chips, 2 * length, hd), bf),
            pltpu.VMEM((2 * n_chips, 2, per, seq), f32),
            pltpu.VMEM((n_chips, length, hd), f32),
            pltpu.VMEM((n_chips, length, hd), f32),
            pltpu.VMEM((2, n_chips, length, hd), bf),
            pltpu.VMEM((2, n_chips, 8, hd), f32),
            pltpu.VMEM((2, n_chips, length, hd), bf),
            pltpu.VMEM((n_chips, 8, hd), f32),
            pltpu.VMEM((2, length, width), bf),
            pltpu.VMEM((2, chunks, rows, part), bf),
            pltpu.VMEM((2, chunks, rows, part), bf),
            pltpu.VMEM((2, chunks, rows, part), bf),
            dma((n_chips // 2, 3)),
            dma,
            dma,
            dma((2,)),
            dma((2,)),
            dma((n_chips, 2)),
            dma((n_chips, 2)),
            dma((n_chips, 2)),
            dma((n_chips, 2)),
            dma((n_chips,)),
            dma((n_chips,)),
            dma((2,)),
            dma((2,)),
            dma,
            dma((n_chips, 2)),
            dma((n_chips, 2)),
            dma((2, n_chips)),
            dma((2, n_chips)),
            dma((n_chips,)),
            dma((n_chips,)),
            dma((2,)),
            dma,
            dma((2, chunks)),
            dma((2, chunks)),
        ],
        compiler_params=pltpu.CompilerParams(
            collective_id=0, has_side_effects=True, vmem_limit_bytes=60 * 1024 * 1024),
        cost_estimate=pl.CostEstimate(flops=6 * 10**9, bytes_accessed=34 * 2**20, transcendentals=3 * 10**6),
    )(tokens_clean, noise_mask, mask_embed, norm_gain, block_mask, jnp.asarray(rotary_table(seq)),
      w_query, w_key, w_value, w_out)
    return pl.pallas_call(
        place_kernel,
        out_shape=(jax.ShapeDtypeStruct((rows, model), bf), jax.ShapeDtypeStruct((rows, model), bf)),
        in_specs=[vmem],
        out_specs=(vmem, vmem),
    )(both)


def fits(mesh, tokens_clean, w_query):
    n_ctx, n_tp = mesh.shape["ctx"], mesh.shape["tp"]
    heads = w_query.shape[1] // n_tp // HEAD_DIM
    tokens = tokens_clean.shape[0] // n_ctx
    return n_tp == 2 and n_ctx == 2 * heads and heads % 4 == 0 and tokens == HEAD_DIM


def solution(mesh):
    specs = dict(
        mesh=mesh,
        in_specs=(
            P(("ctx", "tp"), None),
            P(("ctx", "tp")),
            P(),
            P(),
            P(None, "tp"),
            P(None, "tp"),
            P(None, "tp"),
            P("tp", None),
            P(),
        ),
        out_specs=(P(("ctx", "tp"), None), P(("ctx", "tp"), None)),
        check_vma=False,
    )

    def layer(tokens_clean, noise_mask, mask_embed, norm_gain, w_query, w_key, w_value, w_out, block_mask):
        body = local_kernel if fits(mesh, tokens_clean, w_query) else local
        return jax.shard_map(body, **specs)(
            tokens_clean, noise_mask, mask_embed, norm_gain, w_query, w_key, w_value, w_out, block_mask)

    return layer
```

```python
import functools

import jax
import jax.numpy as jnp
import numpy as np
from jax import lax
from jax.experimental import pallas as pl
from jax.experimental.pallas import tpu as pltpu
from jax.sharding import PartitionSpec as P

HEAD_DIM = 128
BLOCK = 32


ROPE_BASE = 500000.0
EPSILON = 1e-05
NEG_FILL = -1e30


def rms_rows(values, gain):
    wide = values.astype(jnp.float32)
    factor = lax.rsqrt(jnp.mean(wide * wide, axis=-1, keepdims=True) + EPSILON)
    return (wide * factor * gain.astype(jnp.float32)).astype(jnp.bfloat16)


def rotate(values, positions):
    half_dim = values.shape[-1] // 2
    indices = jnp.arange(half_dim).astype(jnp.float32)
    freqs = ROPE_BASE ** (-2.0 * indices / values.shape[-1])
    angles = positions.astype(jnp.float32)[:, None] * freqs[None, :]
    cosine = jnp.cos(angles)[:, None, :]
    sine = jnp.sin(angles)[:, None, :]
    lower = values[..., :half_dim]
    upper = values[..., half_dim:]
    return jnp.concatenate([lower * cosine - upper * sine, upper * cosine + lower * sine], axis=-1)


def start_state(heads, length):
    return (
        jnp.full((heads, length), NEG_FILL, jnp.float32),
        jnp.zeros((heads, length), jnp.float32),
        jnp.zeros((heads, length, HEAD_DIM), jnp.float32),
    )


def attend(state, queries, keys, values, visible):
    peak_old, total_old, weighted_old = state
    scores = jnp.einsum(
        "qhd,khd->hqk", queries, keys, preferred_element_type=jnp.float32
    ) * HEAD_DIM ** (-0.5)
    scores = jnp.where(visible[None], scores, NEG_FILL)
    peak_new = jnp.maximum(peak_old, jnp.max(scores, axis=-1))
    weights = jnp.where(visible[None], jnp.exp(scores - peak_new[..., None]), 0.0)
    factor = jnp.exp(peak_old - peak_new)
    total_new = total_old * factor + jnp.sum(weights, axis=-1)
    weighted_new = weighted_old * factor[..., None] + jnp.einsum(
        "hqk,khd->hqd", weights.astype(jnp.bfloat16), values, preferred_element_type=jnp.float32
    )
    return (peak_new, total_new, weighted_new)


def local(
    tokens_clean, noise_mask, mask_embed, norm_gain, w_query, w_key, w_value, w_out, block_mask
):
    normed = rms_rows(tokens_clean, norm_gain)
    mask_row = rms_rows(mask_embed[None, :], norm_gain)
    gathered, noise_flags = (
        lax.all_gather(normed, "tp", axis=0, tiled=True),
        lax.all_gather(noise_mask, "tp", axis=0, tiled=True),
    )
    local_len = gathered.shape[0]
    width = w_query.shape[1]
    heads = width // HEAD_DIM
    first_row = lax.axis_index("ctx") * local_len
    positions = first_row + jnp.arange(local_len, dtype=jnp.int32)
    noisy_rows = (noise_flags == 1)[:, None]

    def project(weight, rotary):
        clean = jnp.dot(gathered, weight, preferred_element_type=jnp.float32)
        masked = jnp.dot(mask_row, weight, preferred_element_type=jnp.float32)
        noisy = jnp.where(noisy_rows, masked, clean)
        clean = clean.reshape(local_len, heads, HEAD_DIM)
        noisy = noisy.reshape(local_len, heads, HEAD_DIM)
        if rotary:
            clean = rotate(clean, positions)
            noisy = rotate(noisy, positions)
        return (clean.astype(jnp.bfloat16), noisy.astype(jnp.bfloat16))

    q_clean, q_noisy = project(w_query, True)
    k_clean, k_noisy = project(w_key, True)
    v_clean, v_noisy = project(w_value, False)
    key_values = jnp.stack([k_clean.reshape(local_len, width), v_clean.reshape(local_len, width)])

    def finish(state):
        weighted = state[2] / state[1][..., None]
        return jnp.transpose(weighted, (1, 0, 2)).reshape(local_len, width).astype(jnp.bfloat16)

    row_table = jnp.take(block_mask, positions // BLOCK, axis=0)
    own_block = (positions // BLOCK)[:, None] == (positions // BLOCK)[None, :]
    noisy_state = attend(start_state(heads, local_len), q_noisy, k_noisy, v_noisy, own_block)
    states = (start_state(heads, local_len), noisy_state)
    piece = lax.all_gather(key_values, "ctx", axis=1, tiled=True)
    count = piece.shape[1]
    visible = jnp.repeat(row_table, BLOCK, axis=1)
    keys = piece[0].reshape(count, heads, HEAD_DIM)
    values = piece[1].reshape(count, heads, HEAD_DIM)
    states = (
        attend(states[0], q_clean, keys, values, visible % 2 == 1),
        attend(states[1], q_noisy, keys, values, visible // 2 == 1),
    )
    attended = jnp.stack([finish(states[0]), finish(states[1])])
    model_width = w_out.shape[1]
    piece = attended
    summed = lax.psum_scatter(
        jnp.einsum("sqc,cd->qsd", piece, w_out, preferred_element_type=jnp.float32)
        .reshape(local_len // lax.axis_size("tp") * lax.axis_size("tp"), 2 * model_width)
        .astype(jnp.bfloat16),
        "tp",
        scatter_dimension=0,
        tiled=True,
    ).astype(jnp.float32)
    result = summed.reshape(summed.shape[0], 2, model_width)
    return (result[:, 0].astype(jnp.bfloat16), result[:, 1].astype(jnp.bfloat16))

LOG2E = 1.4426950408889634
MESH = pl.DeviceIdType.MESH


def layer_kernel(
    n_chips,
    x_ref, flag_ref, mask_ref, gain_ref, vis_ref, table_hbm, wq_hbm, wk_hbm, wv_hbm, wo_hbm,
    out_ref,
    w_s, wo_s, table, lhs0, lhs1, row0, row1, flags, rowall, rowin, mproj, nb, sendq, sendkv, recvq, recvkv, kall, vall, bias,
    oown, lown, obuf, lbuf, oin, lin, att, psend, precv, pown,
    wsem, wosem, tsem, xs, xr, ss, sr, cs, cr, gs, gr, ls, lc, lg, fs, fr, os_, or_, es, er, ol, el, ps, pr,
):
    ctx = lax.axis_index("ctx")
    tp = lax.axis_index("tp")
    chip = ctx // 2
    core = ctx % 2
    rows = x_ref.shape[0]
    length = 2 * rows
    pairs = n_chips // 2
    hd = HEAD_DIM
    seq = 2 * n_chips * length
    per = length // BLOCK
    my_z = chip // 2
    w_hbm = (wq_hbm, wk_hbm, wv_hbm)
    twin = {"tp": 1 - tp}
    sibling = {"ctx": 2 * chip + 1 - core}

    def pair_at(i):
        return (my_z + 2 + i) % pairs

    def w_copy(kind, i):
        cols = pl.ds(pl.multiple_of(pair_at(i) * 2 * hd, 2 * hd), 2 * hd)
        return pltpu.make_async_copy(w_hbm[kind].at[:, cols], w_s.at[kind, :, cols], wsem.at[i, kind])

    def half_rows(half):
        which = tp if half == 0 else 1 - tp
        return pl.ds(pl.multiple_of(which * rows, rows), rows)

    table_copy = pltpu.make_async_copy(table_hbm, table, tsem)
    for i in range(pairs):
        for kind in (1, 2, 0):
            w_copy(kind, i).start()
        if i == 0:
            table_copy.start()
    wo_copy = pltpu.make_async_copy(wo_hbm, wo_s, wosem)
    wo_copy.start()

    barrier = pltpu.get_barrier_semaphore()
    pl.semaphore_signal(barrier, inc=1, device_id=twin, device_id_type=MESH)
    pl.semaphore_signal(barrier, inc=1, device_id=sibling, device_id_type=MESH)
    for d in range(1, n_chips):
        peer = (chip + d) % n_chips
        pl.semaphore_signal(barrier, inc=1, device_id={"ctx": 2 * peer + core}, device_id_type=MESH)

    gain = gain_ref[...].reshape(1, x_ref.shape[1]).astype(jnp.float32)

    def norm(values):
        wide = values.astype(jnp.float32)
        factor = lax.rsqrt(jnp.mean(wide * wide, axis=-1, keepdims=True) + EPSILON)
        return (wide * factor * gain).astype(jnp.bfloat16)

    lhs0[0:rows, :] = norm(x_ref[...])
    lhs0[rows:rows + 16, :] = jnp.broadcast_to(norm(mask_ref[...].reshape(1, x_ref.shape[1])), (16, lhs0.shape[1]))
    flag_row = flag_ref[...].astype(jnp.float32).reshape(1, rows)
    row0[...] = jnp.broadcast_to(jnp.concatenate([flag_row, flag_row], axis=1), row0.shape)

    pl.semaphore_wait(barrier, n_chips + 1)

    def x_copy():
        return pltpu.make_async_remote_copy(
            src_ref=lhs0.at[pl.ds(0, rows)], dst_ref=lhs1, send_sem=xs.at[0], recv_sem=xr.at[0],
            device_id=twin, device_id_type=MESH)

    def flag_copy():
        return pltpu.make_async_remote_copy(
            src_ref=row0, dst_ref=row1, send_sem=xs.at[1], recv_sem=xr.at[1],
            device_id=twin, device_id_type=MESH)

    flag_copy().start()
    x_copy().start()

    def kv_copy(head, slot, half):
        where = half_rows(half)
        return pltpu.make_async_remote_copy(
            src_ref=sendkv.at[head, where], dst_ref=recvkv.at[slot, where],
            send_sem=ss.at[head, half], recv_sem=sr.at[slot, half],
            device_id={"ctx": 2 * head + core}, device_id_type=MESH)

    def clean_copy(head, slot, half):
        where = half_rows(half)
        return pltpu.make_async_remote_copy(
            src_ref=sendq.at[0, head, where], dst_ref=recvq.at[0, slot, where],
            send_sem=cs.at[head, half], recv_sem=cr.at[slot, half],
            device_id={"ctx": 2 * head + core}, device_id_type=MESH)

    def row_copy(head, slot):
        return pltpu.make_async_remote_copy(
            src_ref=rowall, dst_ref=rowin.at[slot], send_sem=gs.at[head], recv_sem=gr.at[slot],
            device_id={"ctx": 2 * head + core}, device_id_type=MESH)

    def kv_here(half):
        where = half_rows(half)
        return pltpu.make_async_copy(sendkv.at[chip, where], recvkv.at[chip, where], ls.at[half])

    def clean_here(half):
        where = half_rows(half)
        return pltpu.make_async_copy(sendq.at[0, chip, where], recvq.at[0, chip, where], lc.at[half])

    def row_here():
        return pltpu.make_async_copy(rowall, rowin.at[chip], lg)

    def column(row):
        return jnp.transpose(jnp.broadcast_to(row, (length, length)))

    flag_copy().wait_recv()
    lane = lax.broadcasted_iota(jnp.int32, row0.shape, 1)
    rowall[...] = jnp.where(lane // rows == tp, row0[...], row1[...])
    for d in range(1, n_chips):
        row_copy((chip + d) % n_chips, chip).start()
    row_here().start()
    flags[...] = column(rowall[0:1])

    table_copy.wait()
    for half in range(2):
        if half == 1:
            key_at = lax.broadcasted_iota(jnp.int32, (vis_ref.shape[1], seq), 1)
            side = (key_at % (2 * length)) // length
            key_ctx = 2 * (key_at // (2 * length)) + jnp.where(side == 0, core, 1 - core)
            key_block = key_ctx * per + (key_at % length) // BLOCK
            spread = (lax.broadcasted_iota(jnp.int32, key_at.shape, 0) == key_block).astype(jnp.float32).astype(jnp.bfloat16)
            for copy in range(2):
                seen = ((vis_ref[...] >> copy) & 1).astype(jnp.float32).astype(jnp.bfloat16)
                shown = (jnp.dot(seen, spread, preferred_element_type=jnp.float32) - 1.0) * 1e30
                for c in range(2 * n_chips):
                    bias[c, copy] = shown[c * per:(c + 1) * per]
            x_copy().wait_recv()
        where = half_rows(half)

        def project(i, carry):
            pair = pair_at(i)
            cols = pl.ds(pl.multiple_of(pair * 2 * hd, 2 * hd), 2 * hd)
            if half == 0:
                for kind in range(3):
                    w_copy(kind, i).wait()
            flag = flags[where]
            token_rows = pl.ds(pl.multiple_of(ctx * length + (tp if half == 0 else 1 - tp) * rows, rows), rows)
            cosine = table[0, token_rows]
            sine = table[1, token_rows]
            for kind in (1, 2, 0):
                left = (lhs0 if half == 0 else lhs1)[...]
                result = jnp.dot(left, w_s[kind, :, cols], preferred_element_type=jnp.float32)
                if half == 0:
                    mproj[kind, :, cols] = result[rows:rows + 8]
                    masked = result[rows:rows + 1]
                else:
                    masked = mproj[kind, :, cols][0:1]
                clean2 = result[0:rows]
                for k in range(2):
                    head = 2 * pair + k
                    clean = clean2[:, k * hd:(k + 1) * hd]
                    noisy = jnp.where(flag == 1.0, masked[:, k * hd:(k + 1) * hd], clean)
                    if kind < 2:
                        clean = clean * cosine + pltpu.roll(clean, hd // 2, 1) * sine
                        noisy = noisy * cosine + pltpu.roll(noisy, hd // 2, 1) * sine
                    clean = clean.astype(jnp.bfloat16)
                    noisy = noisy.astype(jnp.bfloat16)
                    if kind == 0:
                        sendq[0, head, where, :] = clean
                        sendq[1, head, where, :] = noisy
                    else:
                        nb[kind - 1, head, where, :] = noisy
                        sendkv[head, where, (kind - 1) * hd:kind * hd] = clean
                if kind != 1:
                    for k in range(2):
                        head = 2 * pair + k

                        @pl.when(head != chip)
                        def _():
                            (clean_copy if kind == 0 else kv_copy)(head, chip, half).start()

                        @pl.when(head == chip)
                        def _():
                            (clean_here if kind == 0 else kv_here)(half).start()
            return carry

        lax.fori_loop(0, pairs, project, 0)

    scale = LOG2E * hd ** -0.5
    own = (lax.broadcasted_iota(jnp.int32, (length, length), 0) // BLOCK
           == lax.broadcasted_iota(jnp.int32, (length, length), 1) // BLOCK)

    def dot_t(a, b):
        return lax.dot_general(a, b, (((1,), (1,)), ((), ())), preferred_element_type=jnp.float32)

    for head in range(n_chips):
        scores = jnp.where(own, dot_t(sendq[1, head], nb[0, head]) * scale, NEG_FILL)
        peak = jnp.max(scores, axis=-1, keepdims=True)
        weights = jnp.exp2(scores - peak)
        total = jnp.sum(weights, axis=-1, keepdims=True)
        oown[head] = jnp.dot(weights.astype(jnp.bfloat16), nb[1, head], preferred_element_type=jnp.float32) / total
        lown[head] = jnp.broadcast_to(peak + jnp.log(total) * LOG2E, (length, hd))

    def share(p, kind):
        return pltpu.make_async_remote_copy(
            src_ref=recvkv.at[p, :, pl.ds(kind * hd, hd)],
            dst_ref=(kall, vall)[kind].at[p, pl.ds(length, length)],
            send_sem=fs.at[p, kind], recv_sem=fr.at[p, kind],
            device_id=sibling, device_id_type=MESH)

    def back(p, copy, slot):
        return pltpu.make_async_remote_copy(
            src_ref=obuf.at[copy, p], dst_ref=oin.at[copy, slot], send_sem=os_.at[copy, p], recv_sem=or_.at[copy, slot],
            device_id={"ctx": 2 * p + core}, device_id_type=MESH)

    def level_back(p, slot):
        return pltpu.make_async_remote_copy(
            src_ref=lbuf.at[1, p], dst_ref=lin.at[slot], send_sem=es.at[p], recv_sem=er.at[slot],
            device_id={"ctx": 2 * p + core}, device_id_type=MESH)

    def back_here(copy):
        return pltpu.make_async_copy(obuf.at[copy, chip], oin.at[copy, chip], ol.at[copy])

    def level_here():
        return pltpu.make_async_copy(lbuf.at[1, chip], lin.at[chip], el)

    for p in range(n_chips):
        for half in range(2):
            @pl.when(chip != p)
            def _():
                kv_copy(p, p, half).wait_recv()

            @pl.when(chip == p)
            def _():
                kv_here(half).wait()
        for kind in range(2):
            share(p, kind).start()
        kall[p, 0:length, :] = recvkv[p, :, 0:hd]
        vall[p, 0:length, :] = recvkv[p, :, hd:2 * hd]
    for p in range(n_chips):
        for kind in range(2):
            share(p, kind).wait_recv()

    chunks = psend.shape[1]
    width = psend.shape[3]

    def term_copy(copy, j):
        return pltpu.make_async_remote_copy(
            src_ref=psend.at[copy, j], dst_ref=precv.at[copy, j], send_sem=ps.at[copy, j], recv_sem=pr.at[copy, j],
            device_id=twin, device_id_type=MESH)

    def out_cols(j):
        return pl.ds(pl.multiple_of(j * width, width), width)

    def project_out(copy):
        mine = half_rows(0)
        theirs = half_rows(1)
        for head in range(n_chips):
            @pl.when(chip != head)
            def _():
                back(head, copy, head).wait_recv()

            @pl.when(chip == head)
            def _():
                back_here(copy).wait()
            if copy == 1:
                @pl.when(chip != head)
                def _():
                    level_back(head, head).wait_recv()

                @pl.when(chip == head)
                def _():
                    level_here().wait()
                away = jnp.transpose(jnp.broadcast_to(lin[head][0:1], (length, hd)))
                home = lown[head]
                top = jnp.maximum(away, home)
                w_away = jnp.exp2(away - top)
                w_home = jnp.exp2(home - top)
                noisy = oin[1, head].astype(jnp.float32)
                noisy = (noisy * w_away + oown[head] * w_home) / (w_away + w_home)
                oin[1, head] = noisy.astype(jnp.bfloat16)
            cols = slice(head * hd, (head + 1) * hd)
            att[copy, 0:rows, cols] = oin[copy, head, theirs, :]
            att[copy, rows:length, cols] = oin[copy, head, mine, :]

        def term(j, carry):
            both = jnp.dot(att[copy], wo_s[:, out_cols(j)], preferred_element_type=jnp.float32).astype(jnp.bfloat16)
            psend[copy, j] = both[0:rows]
            pown[copy, j] = both[rows:length]
            term_copy(copy, j).start()
            return carry

        lax.fori_loop(0, chunks, term, 0)

    def attend_step(step, carry):
        copy = step // pairs
        low = (my_z + step) % pairs
        chosen = (low, n_chips - 1 - low)
        for p in chosen:
            @pl.when((copy == 0) & (chip != p))
            def _():
                for half in range(2):
                    clean_copy(p, p, half).wait_recv()
                row_copy(p, p).wait_recv()

            @pl.when((copy == 0) & (chip == p))
            def _():
                for half in range(2):
                    clean_here(half).wait()
                row_here().wait()

            @pl.when(copy == 1)
            def _():
                token_rows = pl.ds(pl.multiple_of((2 * p + core) * length, length), length)
                masked = jnp.broadcast_to(mproj[0, :, pl.ds(pl.multiple_of(chip * hd, hd), hd)][0:1], (length, hd))
                masked = masked * table[0, token_rows] + pltpu.roll(masked, hd // 2, 1) * table[1, token_rows]
                clean = recvq[0, p].astype(jnp.float32)
                recvq[1, p] = jnp.where(column(rowin[p][0:1]) == 1.0, masked, clean).astype(jnp.bfloat16)

        for k in range(pairs):
            @pl.when(low == k)
            def _():
                for q in (k, n_chips - 1 - k):
                    count = (q + 1) * 2 * length
                    keys = kall[0:q + 1].reshape(count, hd)
                    values = vall[0:q + 1].reshape(count, hd)
                    shown = bias[2 * q + core, copy][:, 0:count]
                    extra = jnp.concatenate(
                        [jnp.broadcast_to(shown[b:b + 1], (BLOCK, count)) for b in range(per)], axis=0)
                    scores = dot_t(recvq[copy, q], keys) * scale + extra
                    peak = jnp.max(scores, axis=-1, keepdims=True)
                    weights = jnp.exp2(scores - peak)
                    total = jnp.sum(weights, axis=-1, keepdims=True)
                    result = jnp.dot(weights.astype(jnp.bfloat16), values, preferred_element_type=jnp.float32) / total
                    obuf[copy, q] = result.astype(jnp.bfloat16)
                    level = jnp.broadcast_to(peak + jnp.log(total) * LOG2E, (length, hd))
                    lbuf[copy, q] = jnp.transpose(level)[0:8]

        for p in chosen:
            @pl.when(chip != p)
            def _():
                back(p, copy, chip).start()

            @pl.when(chip == p)
            def _():
                back_here(copy).start()

            @pl.when((copy == 1) & (chip != p))
            def _():
                level_back(p, chip).start()

            @pl.when((copy == 1) & (chip == p))
            def _():
                level_here().start()

        @pl.when(step == pairs + pairs // 2 - 1)
        def _():
            wo_copy.wait()
            project_out(0)
        return carry

    lax.fori_loop(0, 2 * pairs, attend_step, 0)
    project_out(1)

    for copy in range(2):
        def total_of(j, carry):
            term_copy(copy, j).wait_recv()
            summed = pown[copy, j].astype(jnp.float32) + precv[copy, j].astype(jnp.float32)
            out_ref[copy, :, out_cols(j)] = summed.astype(jnp.bfloat16)
            return carry

        lax.fori_loop(0, chunks, total_of, 0)

    flag_copy().wait_send()
    x_copy().wait_send()
    for p in range(n_chips):
        for kind in range(2):
            share(p, kind).wait_send()

        @pl.when(chip != p)
        def _():
            for half in range(2):
                kv_copy(p, chip, half).wait_send()
                clean_copy(p, chip, half).wait_send()
            row_copy(p, chip).wait_send()
            for copy in range(2):
                back(p, copy, chip).wait_send()
            level_back(p, chip).wait_send()
    for copy in range(2):
        for j in range(chunks):
            term_copy(copy, j).wait_send()


def place_kernel(both, clean, noisy):
    clean[...] = both[0]
    noisy[...] = both[1]


def rotary_table(length):
    indices = np.arange(HEAD_DIM // 2).astype(np.float32)
    freqs = (ROPE_BASE ** (-2.0 * indices.astype(np.float64) / HEAD_DIM)).astype(np.float32)
    angles = (np.arange(length, dtype=np.float32)[:, None] * freqs[None, :]).astype(np.float64)
    cosine = np.cos(angles).astype(np.float32)
    sine = np.sin(angles).astype(np.float32)
    return np.stack([np.concatenate([cosine, cosine], axis=1), np.concatenate([-sine, sine], axis=1)])


def local_kernel(
    tokens_clean, noise_mask, mask_embed, norm_gain, w_query, w_key, w_value, w_out, block_mask
):
    rows, model = tokens_clean.shape
    length = 2 * rows
    width = w_query.shape[1]
    n_chips = width // HEAD_DIM
    hd = HEAD_DIM
    seq = 2 * n_chips * length
    per = length // BLOCK
    bf, f32 = jnp.bfloat16, jnp.float32
    chunks = 8
    part = model // chunks
    dma = pltpu.SemaphoreType.DMA
    vmem = pl.BlockSpec(memory_space=pltpu.VMEM)
    hbm = pl.BlockSpec(memory_space=pl.ANY)
    both = pl.pallas_call(
        functools.partial(layer_kernel, n_chips),
        out_shape=jax.ShapeDtypeStruct((2, rows, model), bf),
        in_specs=[vmem] * 5 + [hbm] * 5,
        out_specs=vmem,
        scratch_shapes=[
            pltpu.VMEM((3, model, width), bf),
            pltpu.VMEM((width, model), bf),
            pltpu.VMEM((2, seq, hd), f32),
            pltpu.VMEM((rows + 16, model), bf),
            pltpu.VMEM((rows, model), bf),
            pltpu.VMEM((8, length), f32),
            pltpu.VMEM((8, length), f32),
            pltpu.VMEM((length, hd), f32),
            pltpu.VMEM((8, length), f32),
            pltpu.VMEM((n_chips, 8, length), f32),
            pltpu.VMEM((3, 8, width), f32),
            pltpu.VMEM((2, n_chips, length, hd), bf),
            pltpu.VMEM((2, n_chips, length, hd), bf),
            pltpu.VMEM((n_chips, length, 2 * hd), bf),
            pltpu.VMEM((2, n_chips, length, hd), bf),
            pltpu.VMEM((n_chips, length, 2 * hd), bf),
            pltpu.VMEM((n_chips, 2 * length, hd), bf),
            pltpu.VMEM((n_chips, 2 * length, hd), bf),
            pltpu.VMEM((2 * n_chips, 2, per, seq), f32),
            pltpu.VMEM((n_chips, length, hd), f32),
            pltpu.VMEM((n_chips, length, hd), f32),
            pltpu.VMEM((2, n_chips, length, hd), bf),
            pltpu.VMEM((2, n_chips, 8, hd), f32),
            pltpu.VMEM((2, n_chips, length, hd), bf),
            pltpu.VMEM((n_chips, 8, hd), f32),
            pltpu.VMEM((2, length, width), bf),
            pltpu.VMEM((2, chunks, rows, part), bf),
            pltpu.VMEM((2, chunks, rows, part), bf),
            pltpu.VMEM((2, chunks, rows, part), bf),
            dma((n_chips // 2, 3)),
            dma,
            dma,
            dma((2,)),
            dma((2,)),
            dma((n_chips, 2)),
            dma((n_chips, 2)),
            dma((n_chips, 2)),
            dma((n_chips, 2)),
            dma((n_chips,)),
            dma((n_chips,)),
            dma((2,)),
            dma((2,)),
            dma,
            dma((n_chips, 2)),
            dma((n_chips, 2)),
            dma((2, n_chips)),
            dma((2, n_chips)),
            dma((n_chips,)),
            dma((n_chips,)),
            dma((2,)),
            dma,
            dma((2, chunks)),
            dma((2, chunks)),
        ],
        compiler_params=pltpu.CompilerParams(
            collective_id=0, has_side_effects=True, vmem_limit_bytes=60 * 1024 * 1024),
        cost_estimate=pl.CostEstimate(flops=6 * 10**9, bytes_accessed=34 * 2**20, transcendentals=3 * 10**6),
    )(tokens_clean, noise_mask, mask_embed, norm_gain, block_mask, jnp.asarray(rotary_table(seq)),
      w_query, w_key, w_value, w_out)
    return pl.pallas_call(
        place_kernel,
        out_shape=(jax.ShapeDtypeStruct((rows, model), bf), jax.ShapeDtypeStruct((rows, model), bf)),
        in_specs=[vmem],
        out_specs=(vmem, vmem),
    )(both)


def fits(mesh, tokens_clean, w_query):
    n_ctx, n_tp = mesh.shape["ctx"], mesh.shape["tp"]
    heads = w_query.shape[1] // n_tp // HEAD_DIM
    tokens = tokens_clean.shape[0] // n_ctx
    return n_tp == 2 and n_ctx == 2 * heads and heads % 4 == 0 and tokens == HEAD_DIM


def solution(mesh):
    specs = dict(
        mesh=mesh,
        in_specs=(
            P(("ctx", "tp"), None),
            P(("ctx", "tp")),
            P(),
            P(),
            P(None, "tp"),
            P(None, "tp"),
            P(None, "tp"),
            P("tp", None),
            P(),
        ),
        out_specs=(P(("ctx", "tp"), None), P(("ctx", "tp"), None)),
        check_vma=False,
    )

    def layer(tokens_clean, noise_mask, mask_embed, norm_gain, w_query, w_key, w_value, w_out, block_mask):
        body = local_kernel if fits(mesh, tokens_clean, w_query) else local
        return jax.shard_map(body, **specs)(
            tokens_clean, noise_mask, mask_embed, norm_gain, w_query, w_key, w_value, w_out, block_mask)

    return layer
```
